768 devices in a mesh: dp: 12 (over z), brick: 64 (over x, y, core).
Axes of the slice: x: 4, y: 8, z: 12, core: 2. Of those that a mesh axis runs over, the one named last changes fastest.
Arguments:
- records: bfloat16 [768, 64, 2, 6144], P(('dp', 'brick')), may hold values from -6 to 6
- positions: int32 [768, 64, 2], P(('dp', 'brick')), may hold values from -1 to 127, as said below
- weight: bfloat16 [2592, 192], P('dp'), may hold values from -0.125 to 0.125
- cotangent: bfloat16 [12, 256, 16, 3072], P('dp', 'brick'), may hold values from -0.0234375 to 0.0234375
Outputs:
- activation: bfloat16 [12, 256, 16, 3072], P('dp', 'brick')
- weight_grad: float32 [2592, 192], P('dp')
The draws below stay inside these ranges and needn't reach their ends.
Inputs may be any that keep to these rules, and one draw needn't show every extreme that they name: Entry [d * 64 + s, o, r] is the brick position in owner o's slab of scene d of the r-th record that source s sends to o, or -1 for an empty slot. The live positions at one owner of one scene are distinct; in every scene some owner has all 128 of its slots filled.
All inputs are finite; a program needn't handle non-finite values.
Results may differ from the reference program's by a relative error of at most 0.0029.
Values may be sent and summed in bfloat16 or wider, within the bound.
No kernel may reach another device: no remote copies, remote signals or barrier semaphores. Data moves between devices by JAX's collectives and lax.ppermute only.
A program may use at most 64 MiB of HBM per device.

```python
from functools import partial
import jax
import jax.numpy as jnp
from jax import lax

C_IN = 96
C_OUT = 192
BS = 4
BX = 2
BY = 8
BZ = 8
NPOS = 128
CAP = 2
RX = 8
RY = 32
RZ = 32
OX = 4
OY = 16
OZ = 16
NOUT = 1024
KROWS = 2592
REC = 6144
NXO = 256
N_DP = 12
N_BRICK = 64


def draw_positions(key, part):
    slots = N_BRICK * CAP

    def one_owner(owner_key, busiest):
        level_key, slot_key, place_key = jax.random.split(owner_key, 3)
        level = jnp.where(busiest, 3, jax.random.randint(level_key, (), 0, 4))
        occupied = slots * jnp.array([1, 2, 4, 8], jnp.int32)[level] // 8
        slot_order = jax.random.permutation(slot_key, slots)
        place_order = jax.random.permutation(place_key, NPOS)
        return jnp.where(slot_order < occupied, place_order[slot_order], -1).astype(jnp.int32)

    def one_scene(scene_key):
        full_key, owners_key = jax.random.split(scene_key, 2)
        chosen = jax.random.randint(full_key, (), 0, N_BRICK)
        owner_keys = jax.random.split(owners_key, N_BRICK)
        return jax.vmap(one_owner)(owner_keys, jnp.arange(N_BRICK) == chosen)
    scene_keys = jax.random.split(jax.random.fold_in(key, 7), N_DP)
    table = jax.vmap(one_scene)(scene_keys)
    table = table.reshape(N_DP, N_BRICK, N_BRICK, CAP).transpose(0, 2, 1, 3)
    return table.reshape(N_DP * N_BRICK, N_BRICK, CAP)


def level_of(own_key, extent, shards, least, high):
    factor_of = 1.0
    for dim, shards_of in shards:
        draws = jax.random.uniform(jax.random.fold_in(jax.random.fold_in(own_key, 6), dim), (shards_of,), jnp.float32, least / len(shards), high / len(shards))
        factor_of = factor_of * jnp.repeat(jnp.exp(draws), extent[dim] // shards_of).reshape((-1,) + (1,) * (len(extent) - 1 - dim))
    return factor_of


def noise(stream_key, dims, spread, limit, cuts=(), kind=jnp.bfloat16):
    entries = spread * jax.random.normal(stream_key, dims, jnp.float32)
    if cuts:
        entries = entries * level_of(stream_key, dims, cuts, -0.22, 0.18)
    return jnp.clip(entries, -limit, limit).astype(kind)


def setup_inputs(seed: int = 0) -> dict:
    key_of = jax.random.split(jax.random.key(seed), 5)
    return {
        "records": noise(key_of[0], (N_DP * N_BRICK, N_BRICK, CAP, REC), 1.0, 6.0, ((0, 768),)),
        "positions": draw_positions(jax.random.fold_in(key_of[4], 71), 0),
        "weight": noise(key_of[2], (KROWS, C_OUT), KROWS ** -0.5, 0.125, ((0, 12),)),
        "cotangent": noise(key_of[3], (N_DP, NXO, OY, OZ * C_OUT), 0.004, 0.0234375, ((0, 12), (1, 64))),
    }


def place_records(arrived, places, brick_x, brick_y, brick_z, side, channels):
    count = brick_x * brick_y * brick_z
    target = jnp.where(places >= 0, places, count).astype(jnp.int32)
    filled = jnp.zeros((count + 1, arrived.shape[1]), arrived.dtype).at[target].set(arrived)[:count]
    cubes = filled.reshape(brick_x, brick_y, brick_z, side, side, side, channels)
    cubes = cubes.transpose(0, 3, 1, 4, 2, 5, 6)
    return cubes.reshape(brick_x * side, brick_y * side, brick_z * side, channels)


def columns_of(voxels, boundary):
    padded = jnp.concatenate([boundary, voxels], axis=0)
    padded = jnp.pad(padded, ((0, 0), (1, 0), (1, 0), (0, 0)))
    out_x = voxels.shape[0] // 2
    out_y = voxels.shape[1] // 2
    out_z = voxels.shape[2] // 2
    channels = voxels.shape[3]
    tap_list = []
    for offset_x in range(3):
        for offset_y in range(3):
            for offset_z in range(3):
                tap_list.append(lax.slice(padded, (offset_x, offset_y, offset_z, 0),
                                          (offset_x + 2 * out_x - 1, offset_y + 2 * out_y - 1, offset_z + 2 * out_z - 1, channels),
                                          (2, 2, 2, 1)))
    stacked = jnp.concatenate(tap_list, axis=3)
    return stacked.reshape(out_x * out_y * out_z, 27 * channels)


def layer_terms(columns, weight, upstream):
    linear = jnp.dot(columns, weight, preferred_element_type=jnp.float32)
    activation = jax.nn.silu(linear).astype(jnp.bfloat16)
    sigma = jax.nn.sigmoid(linear)
    slope = sigma * (1.0 + linear * (1.0 - sigma))
    slope_grad = (upstream.astype(jnp.float32) * slope).astype(jnp.bfloat16)
    partial_grad = jnp.dot(columns.T, slope_grad, preferred_element_type=jnp.float32)
    return activation, partial_grad


def reference(records, positions, weight, cotangent):
    width = records.shape[-1]
    slots = N_BRICK * CAP
    scene_records = records.reshape(N_DP, N_BRICK, N_BRICK, CAP, width).transpose(0, 2, 1, 3, 4).reshape(N_DP, N_BRICK, slots, width)
    scene_places = positions.reshape(N_DP, N_BRICK, N_BRICK, CAP).transpose(0, 2, 1, 3).reshape(N_DP, N_BRICK, slots)
    scene_upstream = cotangent.reshape(N_DP, N_BRICK, NOUT, C_OUT)
    placer = partial(place_records, brick_x=BX, brick_y=BY, brick_z=BZ, side=BS, channels=C_IN)

    def one_scene(inputs):
        owner_records, owner_places, owner_upstream = inputs
        grids = jax.vmap(placer)(owner_records, owner_places)
        rims = jnp.concatenate([jnp.zeros((1, 1, RY, RZ, C_IN), grids.dtype), grids[:-1, RX - 1:]], axis=0)

        def one_owner(block):
            voxels, boundary, upstream = block
            return layer_terms(columns_of(voxels, boundary), weight, upstream)

        outputs, grads = lax.map(one_owner, (grids, rims, owner_upstream))
        return outputs, jnp.sum(grads, axis=0)

    outputs, grads = lax.map(one_scene, (scene_records, scene_places, scene_upstream))
    activation = outputs.reshape(N_DP, N_BRICK * OX, OY, OZ * C_OUT)
    return activation, jnp.sum(grads, axis=0)
```

```python
import jax
import jax.numpy as jnp
from jax import lax
from jax.experimental import pallas as pl
from jax.experimental.pallas import tpu as pltpu
from jax.sharding import PartitionSpec as P

C_IN = 96
C_OUT = 192
REC = 6144
NPOS = 128
LINE = 384
DEPTH = 512
TAPS = 9
N_DP = 12
N_BRICK = 64
SHARD = 216
SPLIT = 112
PIECE = 6
ROWS = N_BRICK * PIECE
VMEM = pl.BlockSpec(memory_space=pltpu.VMEM)
F32 = jnp.float32
BF16 = jnp.bfloat16


def params():
    return pltpu.CompilerParams(vmem_limit_bytes=56 * 1024 * 1024)


def brick_rows(shape, dim):
    q = lax.broadcasted_iota(jnp.int32, shape, dim)
    return q >> 4, (q >> 3) & 1, q & 7


def rim_kernel(arrived_ref, rim_ref):
    places = arrived_ref[:, REC : REC + NPOS].astype(F32).T
    m = lax.broadcasted_iota(jnp.int32, (64, NPOS), 0)
    wanted = 64 + (m & 7) * 8 + (m >> 3)
    pick = jnp.where(places[:64] == wanted.astype(F32), 1.0, 0.0).astype(BF16)
    rim_ref[...] = jnp.dot(
        pick, arrived_ref[:, 12 * LINE : REC], preferred_element_type=F32
    ).astype(BF16)


def weight_kernel(weight_ref, wide_ref):
    wide_ref[...] = jnp.zeros_like(wide_ref)
    for tap in range(TAPS):
        block = weight_ref[tap * 288 : (tap + 1) * 288, :]
        wide_ref[tap * DEPTH + 32 : tap * DEPTH + 320, 0:C_OUT] = block
        wide_ref[tap * DEPTH + 224 : tap * DEPTH + 512, C_OUT : 2 * C_OUT] = block


def layer_kernel(
    arrived_ref, rim_ref, wide_ref, cotangent_ref, activation_ref, terms_ref,
    columns, linear, upstream, result, slopes, packed,
):
    places = arrived_ref[:, REC : REC + NPOS].astype(F32).T
    bz, bx, by = brick_rows((NPOS, NPOS), 0)
    rz, rx, ry = brick_rows((NPOS, 64), 0)
    m = lax.broadcasted_iota(jnp.int32, (NPOS, 64), 1)

    def picker(sx, sy, sz):
        inside = (bx >= sx) & (by >= sy) & (bz >= sz)
        wanted = jnp.where(inside, (bx - sx) * 64 + (by - sy) * 8 + bz - sz, -2)
        return jnp.where(places == wanted.astype(F32), 1.0, 0.0).astype(BF16)

    def rim_picker(sy, sz):
        inside = (rx == 0) & (ry >= sy) & (rz >= sz)
        wanted = jnp.where(inside, (rz - sz) * 8 + ry - sy, -2)
        return jnp.where(m == wanted, 1.0, 0.0).astype(BF16)

    for sx in range(2):
        for sy in range(2):
            pick = [picker(sx, sy, sz) for sz in range(2)]
            if sx:
                rim_pick = [rim_picker(sy, sz) for sz in range(2)]
            for vx in [3] if sx else range(4):
                for vy in [3] if sy else range(4):
                    at = (vx * 4 + vy) * LINE
                    line = jnp.dot(pick[0], arrived_ref[:, at : at + LINE], preferred_element_type=F32)
                    before = jnp.dot(
                        pick[1], arrived_ref[:, at + 256 : at + LINE], preferred_element_type=F32
                    )
                    if sx:
                        at = vy * LINE
                        line += jnp.dot(
                            rim_pick[0], rim_ref[:, at : at + LINE], preferred_element_type=F32
                        )
                        before += jnp.dot(
                            rim_pick[1], rim_ref[:, at + 256 : at + LINE], preferred_element_type=F32
                        )
                    line = line.astype(BF16)
                    before = before.astype(BF16)
                    ux = vx - 4 * sx
                    uy = vy - 4 * sy
                    for i in range(2):
                        for j in range(2):
                            a = ux + 1 - 2 * i
                            b = uy + 1 - 2 * j
                            if 0 <= a <= 2 and 0 <= b <= 2:
                                row = (i * 2 + j) * NPOS
                                col = (a * 3 + b) * DEPTH
                                columns[row : row + NPOS, col : col + 128] = before
                                columns[row : row + NPOS, col + 128 : col + DEPTH] = line

    linear[...] = jnp.dot(columns[...], wide_ref[...], preferred_element_type=F32)
    for tile in range(24):
        for x in range(4):
            upstream[x, tile] = cotangent_ref[x, :, tile * 128 : (tile + 1) * 128].astype(F32)
    for i in range(2):
        for j in range(2):
            for z in range(8):
                row = (i * 2 + j) * NPOS + z * 16
                value = linear[row : row + 16, :]
                sigma = 1.0 / (1.0 + jnp.exp(-value))
                active = value * sigma
                slope = sigma * (1.0 + value * (1.0 - sigma))
                incoming = []
                for tile in range(3):
                    lanes = slice(tile * 128, (tile + 1) * 128)
                    parts = []
                    for x in range(2):
                        at = (x * 2 + i, z * 3 + tile, pl.ds(j, 8, stride=2), slice(None))
                        parts.append(upstream[at])
                        result[at] = active[x * 8 : x * 8 + 8, lanes]
                    incoming.append(jnp.concatenate(parts, axis=0))
                incoming = jnp.concatenate(incoming, axis=1)
                slopes[row : row + 16, :] = (incoming * slope).astype(BF16)
    for tile in range(24):
        for x in range(4):
            activation_ref[x, :, tile * 128 : (tile + 1) * 128] = result[x, tile].astype(BF16)

    for d in range(N_DP):
        packed[d * ROWS + SHARD + SPLIT - 8 : (d + 1) * ROWS, :] = jnp.zeros(
            (ROWS - SHARD - SPLIT + 8, 128), F32
        )
    for tap in range(TAPS):
        product = lax.dot_general(
            columns[:, tap * DEPTH : (tap + 1) * DEPTH], slopes[...],
            (((0,), (0,)), ((), ())), preferred_element_type=F32,
        )
        block = product[32:320, 0:C_OUT] + product[224:512, C_OUT : 2 * C_OUT]
        start = tap * 288
        while start < (tap + 1) * 288:
            d, row = divmod(start, SHARD)
            stop = min((tap + 1) * 288, d * SHARD + (SPLIT if row < SPLIT else SHARD))
            part = block[start - tap * 288 : stop - tap * 288]
            size = stop - start
            to = d * ROWS + row
            packed[to : to + size, :] = part[:, 0:128]
            if row < SPLIT:
                packed[to + SHARD : to + SHARD + size, 0:64] = part[:, 128:C_OUT]
            else:
                to = to + SHARD - SPLIT
                packed[to : to + size, 64:128] = part[:, 128:C_OUT]
            start = stop
    for piece in range(N_BRICK):
        terms_ref[piece] = packed[pl.ds(piece, N_DP * PIECE, stride=N_BRICK), :].astype(BF16)


def brick_sum_kernel(terms_ref, sums_ref):
    total = terms_ref[0].astype(F32)
    for source in range(1, N_BRICK):
        total += terms_ref[source].astype(F32)
    for d in range(N_DP):
        sums_ref[d] = total[d * PIECE : (d + 1) * PIECE]


def scene_sum_kernel(sums_ref, copies_ref):
    total = sums_ref[0]
    for source in range(1, N_DP):
        total += sums_ref[source]
    for target in range(N_BRICK):
        copies_ref[target] = total


def unpack_kernel(pieces_ref, grad_ref, packed):
    for row in range(PIECE):
        packed[row * N_BRICK : (row + 1) * N_BRICK, :] = pieces_ref[:, row, :]
    grad_ref[:, 0:128] = packed[0:SHARD, :]
    grad_ref[0:SPLIT, 128:C_OUT] = packed[SHARD : SHARD + SPLIT, 0:64]
    grad_ref[SPLIT:SHARD, 128:C_OUT] = packed[SHARD : 2 * SHARD - SPLIT, 64:128]


def call(kernel, out, scratch=(), count=1):
    return pl.pallas_call(
        kernel,
        out_shape=out,
        in_specs=[VMEM] * count,
        out_specs=jax.tree.map(lambda _: VMEM, out),
        scratch_shapes=list(scratch),
        compiler_params=params(),
    )


def spread(block, axis):
    return lax.all_to_all(block, axis, split_axis=0, concat_axis=0, tiled=True)


def body(records, positions, weight, cotangent):
    shape = jax.ShapeDtypeStruct
    places = jnp.broadcast_to(positions.astype(BF16)[..., None], positions.shape + (NPOS,))
    sent = jnp.concatenate([records, places], axis=3).reshape(N_BRICK, 2, REC + NPOS)
    arrived = spread(sent, "brick").reshape(NPOS, REC + NPOS)
    full_weight = lax.all_gather(weight, "dp", axis=0, tiled=True)
    wide = call(weight_kernel, shape((TAPS * DEPTH, LINE), BF16))(full_weight)
    arrived, wide = lax.optimization_barrier((arrived, wide))
    rim = call(rim_kernel, shape((64, 4 * LINE), BF16))(arrived)
    rim = lax.ppermute(rim, "brick", [(i, i + 1) for i in range(N_BRICK - 1)])
    activation, terms = call(
        layer_kernel,
        (shape((4, 16, 8 * LINE), BF16), shape((N_BRICK, N_DP * PIECE, 128), BF16)),
        [
            pltpu.VMEM((4 * NPOS, TAPS * DEPTH), BF16),
            pltpu.VMEM((4 * NPOS, LINE), F32),
            pltpu.VMEM((4, 24, 16, 128), F32),
            pltpu.VMEM((4, 24, 16, 128), F32),
            pltpu.VMEM((4 * NPOS, LINE), BF16),
            pltpu.VMEM((N_DP * ROWS, 128), F32),
        ],
        4,
    )(arrived, rim, wide, cotangent.reshape(4, 16, 8 * LINE))
    sums = call(brick_sum_kernel, shape((N_DP, PIECE, 128), F32))(spread(terms, "brick"))
    copies = call(scene_sum_kernel, shape((N_BRICK, PIECE, 128), F32))(spread(sums, "dp"))
    grad = call(unpack_kernel, shape((SHARD, C_OUT), F32), [pltpu.VMEM((ROWS, 128), F32)])(
        spread(copies, "brick")
    )
    return activation.reshape(cotangent.shape), grad


def solution(mesh):
    placed = (
        P(("dp", "brick"), None, None, None),
        P(("dp", "brick"), None, None),
        P("dp", None),
        P("dp", "brick", None, None),
    )
    return jax.shard_map(
        body,
        mesh=mesh,
        in_specs=placed,
        out_specs=(P("dp", "brick", None, None), P("dp", None)),
        check_vma=False,
    )
```

```python
import jax
import jax.numpy as jnp
from jax import lax
from jax.experimental import pallas as pl
from jax.experimental.pallas import tpu as pltpu
from jax.sharding import PartitionSpec as P

C_IN = 96
C_OUT = 192
REC = 6144
NPOS = 128
LINE = 384
DEPTH = 512
TAPS = 9
N_DP = 12
N_BRICK = 64
N_CHIP = 32
SHARD = 216
SPLIT = 112
PIECE = 6
ROWS = N_BRICK * PIECE
BRICK = ("x", "y", "core")
ANY = pl.BlockSpec(memory_space=pl.ANY)
VMEM = pl.BlockSpec(memory_space=pltpu.VMEM)
F32 = jnp.float32
BF16 = jnp.bfloat16


def join_kernel(records_ref, places_ref, sent_ref, sems):
    copies = []
    for part in range(8):
        rows = pl.ds(part * 8, 8)
        copies.append(
            pltpu.make_async_copy(
                records_ref.at[rows], sent_ref.at[rows, :, pl.ds(0, REC)], sems.at[part]
            )
        )
    copies.append(
        pltpu.make_async_copy(places_ref, sent_ref.at[:, :, pl.ds(REC, NPOS)], sems.at[8])
    )
    for copy in copies:
        copy.start()
    for copy in copies:
        copy.wait()


def brick_rows(shape, dim):
    q = lax.broadcasted_iota(jnp.int32, shape, dim)
    return q >> 4, (q >> 3) & 1, q & 7


def rim_kernel(tail_ref, rim_ref):
    places = tail_ref[:, 4 * LINE :].astype(F32).T
    m = lax.broadcasted_iota(jnp.int32, (64, NPOS), 0)
    wanted = 64 + (m & 7) * 8 + (m >> 3)
    pick = jnp.where(places[:64] == wanted.astype(F32), 1.0, 0.0).astype(BF16)
    rim_ref[...] = jnp.dot(
        pick, tail_ref[:, 0 : 4 * LINE], preferred_element_type=F32
    ).astype(BF16)


def weight_kernel(weight_ref, wide_ref):
    wide_ref[...] = jnp.zeros_like(wide_ref)
    for tap in range(TAPS):
        block = weight_ref[tap * 288 : (tap + 1) * 288, :]
        wide_ref[tap * DEPTH + 32 : tap * DEPTH + 320, 0:C_OUT] = block
        wide_ref[tap * DEPTH + 224 : tap * DEPTH + 512, C_OUT : 2 * C_OUT] = block


def layer_kernel(
    core_ref, arrived_ref, rim_ref, wide_ref, cotangent_ref, activation_ref, kept_ref, given_ref,
    columns, linear, upstream, result, slopes, packed,
):
    places = arrived_ref[:, REC : REC + NPOS].astype(F32).T
    bz, bx, by = brick_rows((NPOS, NPOS), 0)
    rz, rx, ry = brick_rows((NPOS, 64), 0)
    m = lax.broadcasted_iota(jnp.int32, (NPOS, 64), 1)

    def picker(sx, sy, sz):
        inside = (bx >= sx) & (by >= sy) & (bz >= sz)
        wanted = jnp.where(inside, (bx - sx) * 64 + (by - sy) * 8 + bz - sz, -2)
        return jnp.where(places == wanted.astype(F32), 1.0, 0.0).astype(BF16)

    def rim_picker(sy, sz):
        inside = (rx == 0) & (ry >= sy) & (rz >= sz)
        wanted = jnp.where(inside, (rz - sz) * 8 + ry - sy, -2)
        return jnp.where(m == wanted, 1.0, 0.0).astype(BF16)

    for sx in range(2):
        for sy in range(2):
            pick = [picker(sx, sy, sz) for sz in range(2)]
            if sx:
                rim_pick = [rim_picker(sy, sz) for sz in range(2)]
            for vx in [3] if sx else range(4):
                for vy in [3] if sy else range(4):
                    at = (vx * 4 + vy) * LINE
                    line = jnp.dot(pick[0], arrived_ref[:, at : at + LINE], preferred_element_type=F32)
                    before = jnp.dot(
                        pick[1], arrived_ref[:, at + 256 : at + LINE], preferred_element_type=F32
                    )
                    if sx:
                        at = vy * LINE
                        line += jnp.dot(
                            rim_pick[0], rim_ref[:, at : at + LINE], preferred_element_type=F32
                        )
                        before += jnp.dot(
                            rim_pick[1], rim_ref[:, at + 256 : at + LINE], preferred_element_type=F32
                        )
                    line = line.astype(BF16)
                    before = before.astype(BF16)
                    ux = vx - 4 * sx
                    uy = vy - 4 * sy
                    for i in range(2):
                        for j in range(2):
                            a = ux + 1 - 2 * i
                            b = uy + 1 - 2 * j
                            if 0 <= a <= 2 and 0 <= b <= 2:
                                row = (i * 2 + j) * NPOS
                                col = (a * 3 + b) * DEPTH
                                columns[row : row + NPOS, col : col + 128] = before
                                columns[row : row + NPOS, col + 128 : col + DEPTH] = line

    linear[...] = jnp.dot(columns[...], wide_ref[...], preferred_element_type=F32)
    for tile in range(24):
        for x in range(4):
            upstream[x, tile] = cotangent_ref[x, :, tile * 128 : (tile + 1) * 128].astype(F32)
    for i in range(2):
        for j in range(2):
            for z in range(8):
                row = (i * 2 + j) * NPOS + z * 16
                value = linear[row : row + 16, :]
                sigma = 1.0 / (1.0 + jnp.exp(-value))
                active = value * sigma
                slope = sigma * (1.0 + value * (1.0 - sigma))
                incoming = []
                for tile in range(3):
                    lanes = slice(tile * 128, (tile + 1) * 128)
                    parts = []
                    for x in range(2):
                        at = (x * 2 + i, z * 3 + tile, pl.ds(j, 8, stride=2), slice(None))
                        parts.append(upstream[at])
                        result[at] = active[x * 8 : x * 8 + 8, lanes]
                    incoming.append(jnp.concatenate(parts, axis=0))
                incoming = jnp.concatenate(incoming, axis=1)
                slopes[row : row + 16, :] = (incoming * slope).astype(BF16)
    for tile in range(24):
        for x in range(4):
            activation_ref[x, :, tile * 128 : (tile + 1) * 128] = result[x, tile].astype(BF16)

    for d in range(N_DP):
        packed[d * ROWS + SHARD + SPLIT - 8 : (d + 1) * ROWS, :] = jnp.zeros(
            (ROWS - SHARD - SPLIT + 8, 128), F32
        )
    for tap in range(TAPS):
        product = lax.dot_general(
            columns[:, tap * DEPTH : (tap + 1) * DEPTH], slopes[...],
            (((0,), (0,)), ((), ())), preferred_element_type=F32,
        )
        block = product[32:320, 0:C_OUT] + product[224:512, C_OUT : 2 * C_OUT]
        start = tap * 288
        while start < (tap + 1) * 288:
            d, row = divmod(start, SHARD)
            stop = min((tap + 1) * 288, d * SHARD + (SPLIT if row < SPLIT else SHARD))
            part = block[start - tap * 288 : stop - tap * 288]
            size = stop - start
            to = d * ROWS + row
            packed[to : to + size, :] = part[:, 0:128]
            if row < SPLIT:
                packed[to + SHARD : to + SHARD + size, 0:64] = part[:, 128:C_OUT]
            else:
                to = to + SHARD - SPLIT
                packed[to : to + size, 64:128] = part[:, 128:C_OUT]
            start = stop
    core = core_ref[0]
    for chip in range(N_CHIP):
        kept_ref[chip] = packed[pl.ds(2 * chip + core, N_DP * PIECE, stride=N_BRICK), :]
        given_ref[chip] = packed[pl.ds(2 * chip + 1 - core, N_DP * PIECE, stride=N_BRICK), :]


def chip_sum_kernel(terms_ref, sums_ref):
    total = terms_ref[0].astype(F32)
    for source in range(1, N_CHIP):
        total += terms_ref[source].astype(F32)
    for d in range(N_DP):
        sums_ref[d] = total[d * PIECE : (d + 1) * PIECE]


def scene_sum_kernel(sums_ref, copies_ref):
    total = sums_ref[0]
    for source in range(1, N_DP):
        total += sums_ref[source]
    for target in range(N_BRICK):
        copies_ref[target] = total


def unpack_kernel(pieces_ref, grad_ref, packed):
    for row in range(PIECE):
        packed[row * N_BRICK : (row + 1) * N_BRICK, :] = pieces_ref[:, row, :]
    grad_ref[0:128, :] = packed[0:SHARD, :].T
    grad_ref[128:C_OUT, 0:SPLIT] = packed[SHARD : SHARD + SPLIT, 0:64].T
    grad_ref[128:C_OUT, SPLIT:SHARD] = packed[SHARD : 2 * SHARD - SPLIT, 64:128].T


def call(kernel, out, scratch=(), specs=(VMEM,), out_spec=VMEM, megabytes=8):
    return pl.pallas_call(
        kernel,
        out_shape=out,
        in_specs=list(specs),
        out_specs=jax.tree.map(lambda _: out_spec, out),
        scratch_shapes=list(scratch),
        compiler_params=pltpu.CompilerParams(vmem_limit_bytes=megabytes * 1024 * 1024),
    )


def spread(block, axis):
    return lax.all_to_all(block, axis, split_axis=0, concat_axis=0, tiled=True)


def body(records, positions, weight, cotangent):
    shape = jax.ShapeDtypeStruct
    places = jnp.broadcast_to(positions.astype(BF16)[..., None], positions.shape + (NPOS,))
    sent = call(
        join_kernel, shape((N_BRICK, 2, REC + NPOS), BF16), [pltpu.SemaphoreType.DMA((9,))],
        (ANY, ANY), ANY,
    )(records.reshape(N_BRICK, 2, REC), places.reshape(N_BRICK, 2, NPOS))
    arrived = spread(sent, BRICK).reshape(NPOS, REC + NPOS)
    full_weight = lax.all_gather(weight, "dp", axis=0, tiled=True)
    wide = call(weight_kernel, shape((TAPS * DEPTH, LINE), BF16))(full_weight)
    arrived, wide = lax.optimization_barrier((arrived, wide))
    rim = pl.pallas_call(
        rim_kernel,
        out_shape=shape((64, 4 * LINE), BF16),
        grid=(1,),
        in_specs=[pl.BlockSpec((NPOS, 13 * 128), lambda _: (0, 0))],
        out_specs=pl.BlockSpec((64, 4 * LINE), lambda _: (0, 0)),
        compiler_params=pltpu.CompilerParams(vmem_limit_bytes=8 * 1024 * 1024),
    )(arrived[:, 12 * LINE :])
    rim = lax.ppermute(rim, BRICK, [(i, i + 1) for i in range(N_BRICK - 1)])
    core = lax.axis_index("core").astype(jnp.int32).reshape(1)
    term = shape((N_CHIP, N_DP * PIECE, 128), F32)
    activation, kept, given = call(
        layer_kernel,
        (shape((4, 16, 8 * LINE), BF16), term, term),
        [
            pltpu.VMEM((4 * NPOS, TAPS * DEPTH), BF16),
            pltpu.VMEM((4 * NPOS, LINE), F32),
            pltpu.VMEM((4, 24, 16, 128), F32),
            pltpu.VMEM((4, 24, 16, 128), F32),
            pltpu.VMEM((4 * NPOS, LINE), BF16),
            pltpu.VMEM((N_DP * ROWS, 128), F32),
        ],
        (pl.BlockSpec(memory_space=pltpu.SMEM), VMEM, VMEM, VMEM, VMEM),
        megabytes=28,
    )(core, arrived, rim, wide, cotangent.reshape(4, 16, 8 * LINE))
    taken = lax.ppermute(given, "core", [(0, 1), (1, 0)])
    terms = spread((kept + taken).astype(BF16), ("x", "y"))
    sums = call(chip_sum_kernel, shape((N_DP, PIECE, 128), F32))(terms)
    copies = call(scene_sum_kernel, shape((N_BRICK, PIECE, 128), F32))(spread(sums, "dp"))
    grad = call(unpack_kernel, shape((C_OUT, SHARD), F32), [pltpu.VMEM((ROWS, 128), F32)])(
        spread(copies, BRICK)
    )
    return activation.reshape(cotangent.shape), grad.T


def solution(mesh):
    fine = jax.sharding.Mesh(mesh.devices.reshape(N_DP, 4, 8, 2), ("dp", "x", "y", "core"))
    placed = (
        P(("dp",) + BRICK, None, None, None),
        P(("dp",) + BRICK, None, None),
        P("dp", None),
        P("dp", BRICK, None, None),
    )
    return jax.shard_map(
        body,
        mesh=fine,
        in_specs=placed,
        out_specs=(P("dp", BRICK, None, None), P("dp", None)),
        check_vma=False,
    )
```

```python
import jax
import jax.numpy as jnp
from jax import lax
from jax.experimental import pallas as pl
from jax.experimental.pallas import tpu as pltpu
from jax.sharding import PartitionSpec as P

C_IN = 96
C_OUT = 192
REC = 6144
NPOS = 128
LINE = 384
DEPTH = 512
TAPS = 9
N_DP = 12
N_BRICK = 64
N_CHIP = 32
SHARD = 216
SPLIT = 112
PIECE = 6
ROWS = N_BRICK * PIECE
BRICK = ("x", "y", "core")
HBM = pl.BlockSpec(memory_space=pltpu.HBM)
VMEM = pl.BlockSpec(memory_space=pltpu.VMEM)
F32 = jnp.float32
BF16 = jnp.bfloat16


def join_kernel(records_ref, positions_ref, sent_ref, rows, tile, sems):
    copies = []
    for part in range(8):
        owners = pl.ds(part * 8, 8)
        copies.append(
            pltpu.make_async_copy(
                records_ref.at[owners], sent_ref.at[owners, :, pl.ds(0, REC)], sems.at[part]
            )
        )
    for copy in copies:
        copy.start()
    places = positions_ref[...].astype(F32)
    for slot in range(2):
        rows[pl.ds(slot, N_BRICK, stride=2), :] = jnp.broadcast_to(
            places[slot : slot + 1], (128, N_BRICK)
        ).T
    tile[...] = rows[...].astype(BF16).reshape(N_BRICK, 2, NPOS)
    copies.append(
        pltpu.make_async_copy(tile, sent_ref.at[:, :, pl.ds(REC, NPOS)], sems.at[8])
    )
    copies[8].start()
    for copy in copies:
        copy.wait()


def brick_rows(shape, dim):
    q = lax.broadcasted_iota(jnp.int32, shape, dim)
    return q >> 4, (q >> 3) & 1, q & 7


def rim_kernel(arrived_ref, rim_ref, tail, sem):
    copy = pltpu.make_async_copy(arrived_ref.at[:, :, pl.ds(12 * LINE, 13 * 128)], tail, sem)
    copy.start()
    copy.wait()
    places = tail[:, :, 4 * LINE :].reshape(NPOS, NPOS).astype(F32).T
    m = lax.broadcasted_iota(jnp.int32, (64, NPOS), 0)
    wanted = 64 + (m & 7) * 8 + (m >> 3)
    pick = jnp.where(places[:64] == wanted.astype(F32), 1.0, 0.0).astype(BF16)
    rim_ref[...] = jnp.dot(
        pick, tail[:, :, 0 : 4 * LINE].reshape(NPOS, 4 * LINE), preferred_element_type=F32
    ).astype(BF16)


def weight_kernel(weight_ref, wide_ref):
    wide_ref[...] = jnp.zeros_like(wide_ref)
    for tap in range(TAPS):
        parts = []
        start = tap * 288
        while start < (tap + 1) * 288:
            d, row = divmod(start, SHARD)
            size = min((tap + 1) * 288, (d + 1) * SHARD) - start
            parts.append(weight_ref[d, :, row : row + size])
            start += size
        block = jnp.concatenate(parts, axis=1).T
        wide_ref[tap * DEPTH + 32 : tap * DEPTH + 320, 0:C_OUT] = block
        wide_ref[tap * DEPTH + 224 : tap * DEPTH + 512, C_OUT : 2 * C_OUT] = block


def layer_kernel(
    core_ref, arrived_ref, rim_ref, wide_ref, cotangent_ref, activation_ref, kept_ref, given_ref,
    records, gradient, columns, linear, upstream, result, slopes, packed, sems,
):
    copies = []
    for part, (at, size) in enumerate(
        [(12 * LINE, 4 * LINE + NPOS), (0, 4 * LINE), (4 * LINE, 4 * LINE), (8 * LINE, 4 * LINE)]
    ):
        lanes = pl.ds(at, size)
        copies.append(
            pltpu.make_async_copy(
                arrived_ref.at[:, :, lanes], records.at[:, :, lanes], sems.at[part]
            )
        )
    copies.append(pltpu.make_async_copy(cotangent_ref, gradient, sems.at[4]))
    for copy in copies:
        copy.start()

    def part_of(at, size):
        return records[:, :, at : at + size].reshape(NPOS, size)

    copies[0].wait()
    places = part_of(REC, NPOS).astype(F32).T
    bz, bx, by = brick_rows((NPOS, NPOS), 0)
    rz, rx, ry = brick_rows((NPOS, 64), 0)
    m = lax.broadcasted_iota(jnp.int32, (NPOS, 64), 1)

    def picker(sx, sy, sz):
        inside = (bx >= sx) & (by >= sy) & (bz >= sz)
        wanted = jnp.where(inside, (bx - sx) * 64 + (by - sy) * 8 + bz - sz, -2)
        return jnp.where(places == wanted.astype(F32), 1.0, 0.0).astype(BF16)

    def rim_picker(sy, sz):
        inside = (rx == 0) & (ry >= sy) & (rz >= sz)
        wanted = jnp.where(inside, (rz - sz) * 8 + ry - sy, -2)
        return jnp.where(m == wanted, 1.0, 0.0).astype(BF16)

    for sx in (1, 0):
        for copy in copies[1:4] if sx == 0 else []:
            copy.wait()
        for sy in range(2):
            pick = [picker(sx, sy, sz) for sz in range(2)]
            if sx:
                rim_pick = [rim_picker(sy, sz) for sz in range(2)]
            for vx in [3] if sx else range(4):
                for vy in [3] if sy else range(4):
                    at = (vx * 4 + vy) * LINE
                    source = part_of(at, LINE)
                    line = jnp.dot(pick[0], source, preferred_element_type=F32)
                    before = jnp.dot(pick[1], source[:, 256:], preferred_element_type=F32)
                    if sx:
                        at = vy * LINE
                        line += jnp.dot(
                            rim_pick[0], rim_ref[:, at : at + LINE], preferred_element_type=F32
                        )
                        before += jnp.dot(
                            rim_pick[1], rim_ref[:, at + 256 : at + LINE], preferred_element_type=F32
                        )
                    line = line.astype(BF16)
                    before = before.astype(BF16)
                    ux = vx - 4 * sx
                    uy = vy - 4 * sy
                    for i in range(2):
                        for j in range(2):
                            a = ux + 1 - 2 * i
                            b = uy + 1 - 2 * j
                            if 0 <= a <= 2 and 0 <= b <= 2:
                                row = (i * 2 + j) * NPOS
                                col = (a * 3 + b) * DEPTH
                                columns[row : row + NPOS, col : col + 128] = before
                                columns[row : row + NPOS, col + 128 : col + DEPTH] = line

    linear[...] = jnp.dot(columns[...], wide_ref[...], preferred_element_type=F32)
    copies[4].wait()
    for tile in range(24):
        for x in range(4):
            upstream[x, tile] = gradient[x, :, tile * 128 : (tile + 1) * 128].astype(F32)
    for i in range(2):
        for j in range(2):
            for z in range(8):
                row = (i * 2 + j) * NPOS + z * 16
                value = linear[row : row + 16, :]
                sigma = 1.0 / (1.0 + jnp.exp(-value))
                active = value * sigma
                slope = sigma * (1.0 + value * (1.0 - sigma))
                incoming = []
                for tile in range(3):
                    lanes = slice(tile * 128, (tile + 1) * 128)
                    parts = []
                    for x in range(2):
                        at = (x * 2 + i, z * 3 + tile, pl.ds(j, 8, stride=2), slice(None))
                        parts.append(upstream[at])
                        result[at] = active[x * 8 : x * 8 + 8, lanes]
                    incoming.append(jnp.concatenate(parts, axis=0))
                incoming = jnp.concatenate(incoming, axis=1)
                slopes[row : row + 16, :] = (incoming * slope).astype(BF16)
    for tile in range(24):
        for x in range(4):
            activation_ref[x, :, tile * 128 : (tile + 1) * 128] = result[x, tile].astype(BF16)

    for d in range(N_DP):
        packed[d * ROWS + SHARD + SPLIT - 8 : (d + 1) * ROWS, :] = jnp.zeros(
            (ROWS - SHARD - SPLIT + 8, 128), F32
        )
    for tap in range(TAPS):
        product = lax.dot_general(
            columns[:, tap * DEPTH : (tap + 1) * DEPTH], slopes[...],
            (((0,), (0,)), ((), ())), preferred_element_type=F32,
        )
        block = product[32:320, 0:C_OUT] + product[224:512, C_OUT : 2 * C_OUT]
        start = tap * 288
        while start < (tap + 1) * 288:
            d, row = divmod(start, SHARD)
            stop = min((tap + 1) * 288, d * SHARD + (SPLIT if row < SPLIT else SHARD))
            part = block[start - tap * 288 : stop - tap * 288]
            size = stop - start
            to = d * ROWS + row
            packed[to : to + size, :] = part[:, 0:128]
            if row < SPLIT:
                packed[to + SHARD : to + SHARD + size, 0:64] = part[:, 128:C_OUT]
            else:
                to = to + SHARD - SPLIT
                packed[to : to + size, 64:128] = part[:, 128:C_OUT]
            start = stop
    core = core_ref[0]
    for chip in range(N_CHIP):
        kept_ref[chip] = packed[pl.ds(2 * chip + core, N_DP * PIECE, stride=N_BRICK), :]
        given_ref[chip] = packed[pl.ds(2 * chip + 1 - core, N_DP * PIECE, stride=N_BRICK), :]


def chip_sum_kernel(terms_ref, sums_ref):
    total = terms_ref[0].astype(F32)
    for source in range(1, N_CHIP):
        total += terms_ref[source].astype(F32)
    for d in range(N_DP):
        sums_ref[d] = total[d * PIECE : (d + 1) * PIECE]


def scene_sum_kernel(sums_ref, copies_ref):
    total = sums_ref[0]
    for source in range(1, N_DP):
        total += sums_ref[source]
    for target in range(N_BRICK):
        copies_ref[target] = total


def unpack_kernel(pieces_ref, grad_ref, packed):
    for row in range(PIECE):
        packed[row * N_BRICK : (row + 1) * N_BRICK, :] = pieces_ref[:, row, :]
    grad_ref[0:128, :] = packed[0:SHARD, :].T
    grad_ref[128:C_OUT, 0:SPLIT] = packed[SHARD : SHARD + SPLIT, 0:64].T
    grad_ref[128:C_OUT, SPLIT:SHARD] = packed[SHARD : 2 * SHARD - SPLIT, 64:128].T


def call(kernel, out, scratch=(), specs=(VMEM,), out_spec=VMEM, megabytes=8):
    return pl.pallas_call(
        kernel,
        out_shape=out,
        in_specs=list(specs),
        out_specs=jax.tree.map(lambda _: out_spec, out),
        scratch_shapes=list(scratch),
        compiler_params=pltpu.CompilerParams(vmem_limit_bytes=megabytes * 1024 * 1024),
    )


def spread(block, axis):
    return lax.all_to_all(block, axis, split_axis=0, concat_axis=0, tiled=True)


def body(records, positions, weight, cotangent):
    shape = jax.ShapeDtypeStruct
    sent = call(
        join_kernel,
        shape((N_BRICK, 2, REC + NPOS), BF16),
        [
            pltpu.VMEM((2 * N_BRICK, NPOS), F32),
            pltpu.VMEM((N_BRICK, 2, NPOS), BF16),
            pltpu.SemaphoreType.DMA((9,)),
        ],
        (HBM, VMEM),
        HBM,
    )(records.reshape(N_BRICK, 2, REC), positions.reshape(N_BRICK, 2).T)
    arrived = spread(sent, BRICK)
    full_weight = lax.all_gather(weight.T, "dp", axis=0, tiled=False)
    wide = call(weight_kernel, shape((TAPS * DEPTH, LINE), BF16))(full_weight)
    arrived, wide = lax.optimization_barrier((arrived, wide))
    rim = call(
        rim_kernel,
        shape((64, 4 * LINE), BF16),
        [pltpu.VMEM((N_BRICK, 2, 13 * 128), BF16), pltpu.SemaphoreType.DMA],
        (HBM,),
    )(arrived)
    rim = lax.ppermute(rim, BRICK, [(i, i + 1) for i in range(N_BRICK - 1)])
    core = lax.axis_index("core").astype(jnp.int32).reshape(1)
    term = shape((N_CHIP, N_DP * PIECE, 128), F32)
    activation, kept, given = call(
        layer_kernel,
        (shape((4, 16, 8 * LINE), BF16), term, term),
        [
            pltpu.VMEM((N_BRICK, 2, REC + NPOS), BF16),
            pltpu.VMEM((4, 16, 8 * LINE), BF16),
            pltpu.VMEM((4 * NPOS, TAPS * DEPTH), BF16),
            pltpu.VMEM((4 * NPOS, LINE), F32),
            pltpu.VMEM((4, 24, 16, 128), F32),
            pltpu.VMEM((4, 24, 16, 128), F32),
            pltpu.VMEM((4 * NPOS, LINE), BF16),
            pltpu.VMEM((N_DP * ROWS, 128), F32),
            pltpu.SemaphoreType.DMA((5,)),
        ],
        (pl.BlockSpec(memory_space=pltpu.SMEM), HBM, VMEM, VMEM, HBM),
        megabytes=20,
    )(core, arrived, rim, wide, cotangent.reshape(4, 16, 8 * LINE))
    taken = lax.ppermute(given, "core", [(0, 1), (1, 0)])
    terms = spread((kept + taken).astype(BF16), ("x", "y"))
    sums = call(chip_sum_kernel, shape((N_DP, PIECE, 128), F32))(terms)
    copies = call(scene_sum_kernel, shape((N_BRICK, PIECE, 128), F32))(spread(sums, "dp"))
    grad = call(unpack_kernel, shape((C_OUT, SHARD), F32), [pltpu.VMEM((ROWS, 128), F32)])(
        spread(copies, BRICK)
    )
    return activation.reshape(cotangent.shape), grad.T


def solution(mesh):
    fine = jax.sharding.Mesh(mesh.devices.reshape(N_DP, 4, 8, 2), ("dp", "x", "y", "core"))
    placed = (
        P(("dp",) + BRICK, None, None, None),
        P(("dp",) + BRICK, None, None),
        P("dp", None),
        P("dp", BRICK, None, None),
    )
    return jax.shard_map(
        body,
        mesh=fine,
        in_specs=placed,
        out_specs=(P("dp", BRICK, None, None), P("dp", None)),
        check_vma=False,
    )
```

```python
import jax
import jax.numpy as jnp
from jax import lax
from jax.experimental import pallas as pl
from jax.experimental.pallas import tpu as pltpu
from jax.sharding import PartitionSpec as P

C_IN = 96
C_OUT = 192
REC = 6144
NPOS = 128
LINE = 384
DEPTH = 512
TAPS = 9
N_DP = 12
N_BRICK = 64
N_CHIP = 32
SHARD = 216
SPLIT = 112
PIECE = 6
CHUNKS = 8
ROWS = N_BRICK * PIECE
BRICK = ("x", "y", "core")
HBM = pl.BlockSpec(memory_space=pltpu.HBM)
VMEM = pl.BlockSpec(memory_space=pltpu.VMEM)
F32 = jnp.float32
BF16 = jnp.bfloat16


def join_kernel(records_ref, positions_ref, sent_ref, joined, places, rows, sems):
    size = N_BRICK // CHUNKS
    coming = [pltpu.make_async_copy(positions_ref, places, sems.at[2 * CHUNKS])]
    going = []
    for part in range(CHUNKS):
        owners = pl.ds(part * size, size)
        coming.append(
            pltpu.make_async_copy(
                records_ref.at[owners], joined.at[owners, :, pl.ds(0, REC)], sems.at[part]
            )
        )
        going.append(
            pltpu.make_async_copy(joined.at[owners], sent_ref.at[owners], sems.at[CHUNKS + part])
        )
    for copy in coming:
        copy.start()
    coming[0].wait()
    for slot in range(2):
        rows[pl.ds(slot, N_BRICK, stride=2), :] = jnp.broadcast_to(
            places[slot : slot + 1, :].astype(F32), (128, N_BRICK)
        ).T
    joined[:, :, REC:] = rows[...].astype(BF16).reshape(N_BRICK, 2, NPOS)
    for part in range(CHUNKS):
        coming[1 + part].wait()
        going[part].start()
    for copy in going:
        copy.wait()


def brick_rows(shape, dim):
    q = lax.broadcasted_iota(jnp.int32, shape, dim)
    return q >> 4, (q >> 3) & 1, q & 7


def rim_kernel(arrived_ref, rim_ref):
    places = arrived_ref[:, :, REC:].reshape(NPOS, NPOS).astype(F32).T
    m = lax.broadcasted_iota(jnp.int32, (64, NPOS), 0)
    wanted = 64 + (m & 7) * 8 + (m >> 3)
    pick = jnp.where(places[:64] == wanted.astype(F32), 1.0, 0.0).astype(BF16)
    rim_ref[...] = jnp.dot(
        pick,
        arrived_ref[:, :, 12 * LINE : REC].reshape(NPOS, 4 * LINE),
        preferred_element_type=F32,
    ).astype(BF16)


def widen(weight_ref, wide):
    wide[...] = jnp.zeros_like(wide)
    for tap in range(TAPS):
        parts = []
        start = tap * 288
        while start < (tap + 1) * 288:
            d, row = divmod(start, SHARD)
            size = min((tap + 1) * 288, (d + 1) * SHARD) - start
            parts.append(weight_ref[d, :, row : row + size])
            start += size
        block = jnp.concatenate(parts, axis=1).T
        wide[tap * DEPTH + 32 : tap * DEPTH + 320, 0:C_OUT] = block
        wide[tap * DEPTH + 224 : tap * DEPTH + 512, C_OUT : 2 * C_OUT] = block


def store_line(columns, line, before, ux, uy, width):
    for i in range(2 if width == TAPS else 1):
        for j in range(2):
            a = ux + 1 - 2 * i
            b = uy + 1 - 2 * j
            if 0 <= a <= 2 and 0 <= b <= 2:
                row = (i * 2 + j) * NPOS
                col = (a * 3 + b) * DEPTH
                columns[row : row + NPOS, col : col + 128] = before
                columns[row : row + NPOS, col + 128 : col + DEPTH] = line


def place_kernel(arrived_ref, weight_ref, columns_ref, linear_ref, first_ref, wide):
    widen(weight_ref, wide)
    first_ref[...] = wide[0 : 3 * DEPTH, :]
    places = arrived_ref[:, :, REC:].reshape(NPOS, NPOS).astype(F32).T
    bz, bx, by = brick_rows((NPOS, NPOS), 0)

    def picker(sx, sy, sz):
        inside = (bx >= sx) & (by >= sy) & (bz >= sz)
        wanted = jnp.where(inside, (bx - sx) * 64 + (by - sy) * 8 + bz - sz, -2)
        return jnp.where(places == wanted.astype(F32), 1.0, 0.0).astype(BF16)

    for sx in range(2):
        for sy in range(2):
            pick = [picker(sx, sy, sz) for sz in range(2)]
            for vx in [3] if sx else range(4):
                for vy in [3] if sy else range(4):
                    at = (vx * 4 + vy) * LINE
                    source = arrived_ref[:, :, at : at + LINE].reshape(NPOS, LINE)
                    line = jnp.dot(pick[0], source, preferred_element_type=F32)
                    before = jnp.dot(pick[1], source[:, 256:], preferred_element_type=F32)
                    store_line(
                        columns_ref, line.astype(BF16), before.astype(BF16),
                        vx - 4 * sx, vy - 4 * sy, TAPS,
                    )
    linear_ref[...] = jnp.dot(columns_ref[...], wide[...], preferred_element_type=F32)


def transposed_dot(left, right):
    return lax.dot_general(left, right, (((0,), (0,)), ((), ())), preferred_element_type=F32)


def layer_kernel(
    core_ref, columns_ref, linear_ref, first_ref, rim_ref, cotangent_ref,
    activation_ref, kept_ref, given_ref,
    front, linear, upstream, result, slopes, packed,
):
    rz, rx, ry = brick_rows((NPOS, 64), 0)
    m = lax.broadcasted_iota(jnp.int32, (NPOS, 64), 1)

    def rim_picker(sy, sz):
        inside = (rx == 0) & (ry >= sy) & (rz >= sz)
        wanted = jnp.where(inside, (rz - sz) * 8 + ry - sy, -2)
        return jnp.where(m == wanted, 1.0, 0.0).astype(BF16)

    for sy in range(2):
        pick = [rim_picker(sy, sz) for sz in range(2)]
        for vy in [3] if sy else range(4):
            source = rim_ref[:, vy * LINE : (vy + 1) * LINE]
            line = jnp.dot(pick[0], source, preferred_element_type=F32)
            before = jnp.dot(pick[1], source[:, 256:], preferred_element_type=F32)
            store_line(front, line.astype(BF16), before.astype(BF16), -1, vy - 4 * sy, 3)
    half = 2 * NPOS
    linear[0:half, :] = linear_ref[0:half, :] + jnp.dot(
        front[...], first_ref[...], preferred_element_type=F32
    )
    linear[half:, :] = linear_ref[half:, :]
    front[...] += columns_ref[0:half, 0 : 3 * DEPTH]

    for tile in range(24):
        for x in range(4):
            upstream[x, tile] = cotangent_ref[x, :, tile * 128 : (tile + 1) * 128].astype(F32)
    for i in range(2):
        for j in range(2):
            for z in range(8):
                row = (i * 2 + j) * NPOS + z * 16
                value = linear[row : row + 16, :]
                sigma = 1.0 / (1.0 + jnp.exp(-value))
                active = value * sigma
                slope = sigma * (1.0 + value * (1.0 - sigma))
                incoming = []
                for tile in range(3):
                    lanes = slice(tile * 128, (tile + 1) * 128)
                    parts = []
                    for x in range(2):
                        at = (x * 2 + i, z * 3 + tile, pl.ds(j, 8, stride=2), slice(None))
                        parts.append(upstream[at])
                        result[at] = active[x * 8 : x * 8 + 8, lanes]
                    incoming.append(jnp.concatenate(parts, axis=0))
                incoming = jnp.concatenate(incoming, axis=1)
                slopes[row : row + 16, :] = (incoming * slope).astype(BF16)
    for tile in range(24):
        for x in range(4):
            activation_ref[x, :, tile * 128 : (tile + 1) * 128] = result[x, tile].astype(BF16)

    for d in range(N_DP):
        packed[d * ROWS + SHARD + SPLIT - 8 : (d + 1) * ROWS, :] = jnp.zeros(
            (ROWS - SHARD - SPLIT + 8, 128), F32
        )
    for tap in range(TAPS):
        lanes = slice(tap * DEPTH, (tap + 1) * DEPTH)
        if tap < 3:
            product = transposed_dot(front[:, lanes], slopes[0:half, :]) + transposed_dot(
                columns_ref[half:, lanes], slopes[half:, :]
            )
        else:
            product = transposed_dot(columns_ref[:, lanes], slopes[...])
        block = product[32:320, 0:C_OUT] + product[224:512, C_OUT : 2 * C_OUT]
        start = tap * 288
        while start < (tap + 1) * 288:
            d, row = divmod(start, SHARD)
            stop = min((tap + 1) * 288, d * SHARD + (SPLIT if row < SPLIT else SHARD))
            part = block[start - tap * 288 : stop - tap * 288]
            size = stop - start
            to = d * ROWS + row
            packed[to : to + size, :] = part[:, 0:128]
            if row < SPLIT:
                packed[to + SHARD : to + SHARD + size, 0:64] = part[:, 128:C_OUT]
            else:
                to = to + SHARD - SPLIT
                packed[to : to + size, 64:128] = part[:, 128:C_OUT]
            start = stop
    core = core_ref[0]
    for chip in range(N_CHIP):
        kept_ref[chip] = packed[pl.ds(2 * chip + core, N_DP * PIECE, stride=N_BRICK), :]
        given_ref[chip] = packed[pl.ds(2 * chip + 1 - core, N_DP * PIECE, stride=N_BRICK), :]


def chip_sum_kernel(terms_ref, sums_ref):
    total = terms_ref[0].astype(F32)
    for source in range(1, N_CHIP):
        total += terms_ref[source].astype(F32)
    for d in range(N_DP):
        sums_ref[d] = total[d * PIECE : (d + 1) * PIECE]


def scene_sum_kernel(sums_ref, copies_ref):
    total = sums_ref[0]
    for source in range(1, N_DP):
        total += sums_ref[source]
    for target in range(N_BRICK):
        copies_ref[target] = total


def unpack_kernel(pieces_ref, grad_ref, packed):
    for row in range(PIECE):
        packed[row * N_BRICK : (row + 1) * N_BRICK, :] = pieces_ref[:, row, :]
    grad_ref[0:128, :] = packed[0:SHARD, :].T
    grad_ref[128:C_OUT, 0:SPLIT] = packed[SHARD : SHARD + SPLIT, 0:64].T
    grad_ref[128:C_OUT, SPLIT:SHARD] = packed[SHARD : 2 * SHARD - SPLIT, 64:128].T


def call(kernel, out, scratch=(), specs=(VMEM,), out_spec=VMEM, megabytes=8, flops=0):
    return pl.pallas_call(
        kernel,
        out_shape=out,
        in_specs=list(specs),
        out_specs=jax.tree.map(lambda _: out_spec, out),
        scratch_shapes=list(scratch),
        compiler_params=pltpu.CompilerParams(vmem_limit_bytes=megabytes * 1024 * 1024),
        cost_estimate=pl.CostEstimate(flops=flops, bytes_accessed=0, transcendentals=0) if flops else None,
    )


def spread(block, axis):
    return lax.all_to_all(block, axis, split_axis=0, concat_axis=0, tiled=True)


def body(records, positions, weight, cotangent):
    shape = jax.ShapeDtypeStruct
    sent = call(
        join_kernel,
        shape((N_BRICK, 2, REC + NPOS), BF16),
        [
            pltpu.VMEM((N_BRICK, 2, REC + NPOS), BF16),
            pltpu.VMEM((2, N_BRICK), jnp.int32),
            pltpu.VMEM((2 * N_BRICK, NPOS), F32),
            pltpu.SemaphoreType.DMA((2 * CHUNKS + 1,)),
        ],
        (HBM, HBM),
        HBM,
        61,
    )(records.reshape(N_BRICK, 2, REC), positions.reshape(N_BRICK, 2).T)
    arrived = spread(sent, BRICK)
    full_weight = lax.all_gather(weight.T, "dp", axis=0, tiled=False)
    arrived, full_weight = lax.optimization_barrier((arrived, full_weight))
    rim = call(rim_kernel, shape((64, 4 * LINE), BF16))(arrived)
    rim = lax.ppermute(rim, BRICK, [(i, i + 1) for i in range(N_BRICK - 1)])
    columns, linear, first = call(
        place_kernel,
        (
            shape((4 * NPOS, TAPS * DEPTH), BF16),
            shape((4 * NPOS, LINE), F32),
            shape((3 * DEPTH, LINE), BF16),
        ),
        [pltpu.VMEM((TAPS * DEPTH, LINE), BF16)],
        (VMEM, VMEM),
        megabytes=16,
        flops=2 * 4 * NPOS * TAPS * DEPTH * LINE,
    )(arrived, full_weight)
    core = lax.axis_index("core").astype(jnp.int32).reshape(1)
    term = shape((N_CHIP, N_DP * PIECE, 128), F32)
    activation, kept, given = call(
        layer_kernel,
        (shape((4, 16, 8 * LINE), BF16), term, term),
        [
            pltpu.VMEM((2 * NPOS, 3 * DEPTH), BF16),
            pltpu.VMEM((4 * NPOS, LINE), F32),
            pltpu.VMEM((4, 24, 16, 128), F32),
            pltpu.VMEM((4, 24, 16, 128), F32),
            pltpu.VMEM((4 * NPOS, LINE), BF16),
            pltpu.VMEM((N_DP * ROWS, 128), F32),
        ],
        (pl.BlockSpec(memory_space=pltpu.SMEM),) + (VMEM,) * 5,
        megabytes=16,
    )(core, columns, linear, first, rim, cotangent.reshape(4, 16, 8 * LINE))
    taken = lax.ppermute(given, "core", [(0, 1), (1, 0)])
    terms = spread((kept + taken).astype(BF16), ("x", "y"))
    sums = call(chip_sum_kernel, shape((N_DP, PIECE, 128), F32))(terms)
    copies = call(scene_sum_kernel, shape((N_BRICK, PIECE, 128), F32))(spread(sums, "dp"))
    grad = call(unpack_kernel, shape((C_OUT, SHARD), F32), [pltpu.VMEM((ROWS, 128), F32)])(
        spread(copies, BRICK)
    )
    return activation.reshape(cotangent.shape), grad.T


def solution(mesh):
    fine = jax.sharding.Mesh(mesh.devices.reshape(N_DP, 4, 8, 2), ("dp", "x", "y", "core"))
    placed = (
        P(("dp",) + BRICK, None, None, None),
        P(("dp",) + BRICK, None, None),
        P("dp", None),
        P("dp", BRICK, None, None),
    )
    return jax.shard_map(
        body,
        mesh=fine,
        in_specs=placed,
        out_specs=(P("dp", BRICK, None, None), P("dp", None)),
        check_vma=False,
    )
```

```python
import jax
import jax.numpy as jnp
from jax import lax
from jax.experimental import pallas as pl
from jax.experimental.pallas import tpu as pltpu
from jax.sharding import PartitionSpec as P

C_IN = 96
C_OUT = 192
REC = 6144
NPOS = 128
LINE = 384
DEPTH = 512
TAPS = 9
N_DP = 12
N_BRICK = 64
N_CHIP = 32
SHARD = 216
SPLIT = 112
KEEP = 104
PIECE = 5
TERM = 64
CHUNKS = 8
WIDTH = (PIECE + 1) * 128
ROWS = N_BRICK * PIECE
BRICK = ("x", "y", "core")
HBM = pl.BlockSpec(memory_space=pltpu.HBM)
VMEM = pl.BlockSpec(memory_space=pltpu.VMEM)
F32 = jnp.float32
BF16 = jnp.bfloat16


def join_kernel(records_ref, positions_ref, sent_ref, staged, tile, places, rows, sems):
    size = N_BRICK // CHUNKS
    coming = [pltpu.make_async_copy(positions_ref, places, sems.at[2 * CHUNKS])]
    going = []
    for part in range(CHUNKS):
        owners = pl.ds(part * size, size)
        coming.append(
            pltpu.make_async_copy(
                records_ref.at[owners], staged.at[owners], sems.at[part]
            )
        )
        going.append(
            pltpu.make_async_copy(
                staged.at[owners], sent_ref.at[owners, :, pl.ds(0, REC)], sems.at[CHUNKS + part]
            )
        )
    for copy in coming:
        copy.start()
    going.append(
        pltpu.make_async_copy(
            tile, sent_ref.at[:, :, pl.ds(REC, NPOS)], sems.at[2 * CHUNKS + 1]
        )
    )
    coming[0].wait()
    for slot in range(2):
        rows[pl.ds(slot, N_BRICK, stride=2), :] = jnp.broadcast_to(
            places[slot : slot + 1, :].astype(F32), (128, N_BRICK)
        ).T
    tile[...] = rows[...].astype(BF16).reshape(N_BRICK, 2, NPOS)
    going[CHUNKS].start()
    for part in range(CHUNKS):
        coming[1 + part].wait()
        going[part].start()
    for copy in going:
        copy.wait()


def brick_rows(shape, dim):
    q = lax.broadcasted_iota(jnp.int32, shape, dim)
    return q >> 4, (q >> 3) & 1, q & 7


def rim_kernel(arrived_ref, rim_ref):
    places = arrived_ref[:, :, REC:].reshape(NPOS, NPOS).astype(F32).T
    m = lax.broadcasted_iota(jnp.int32, (64, NPOS), 0)
    wanted = 64 + (m & 7) * 8 + (m >> 3)
    pick = jnp.where(places[:64] == wanted.astype(F32), 1.0, 0.0).astype(BF16)
    rim_ref[...] = jnp.dot(
        pick,
        arrived_ref[:, :, 12 * LINE : REC].reshape(NPOS, 4 * LINE),
        preferred_element_type=F32,
    ).astype(BF16)


def weight_kernel(weight_ref, tall_ref):
    for tap in range(TAPS):
        parts = []
        start = tap * 288
        while start < (tap + 1) * 288:
            d, row = divmod(start, SHARD)
            size = min((tap + 1) * 288, (d + 1) * SHARD) - start
            parts.append(weight_ref[d, :, row : row + size])
            start += size
        tall_ref[tap * 288 : (tap + 1) * 288, :] = jnp.concatenate(parts, axis=1).T


def widen(tall_ref, wide):
    for tap in range(TAPS):
        at = tap * DEPTH
        block = tall_ref[tap * 288 : (tap + 1) * 288, :]
        wide[at : at + 32, 0:C_OUT] = jnp.zeros((32, C_OUT), BF16)
        wide[at + 32 : at + 320, 0:C_OUT] = block
        wide[at + 320 : at + 512, 0:C_OUT] = jnp.zeros((192, C_OUT), BF16)
        wide[at : at + 224, C_OUT:] = jnp.zeros((224, C_OUT), BF16)
        wide[at + 224 : at + 512, C_OUT:] = block


def store_line(columns, line, before, ux, uy, width):
    for i in range(2 if width == TAPS else 1):
        for j in range(2):
            a = ux + 1 - 2 * i
            b = uy + 1 - 2 * j
            if 0 <= a <= 2 and 0 <= b <= 2:
                row = (i * 2 + j) * NPOS
                col = (a * 3 + b) * DEPTH
                columns[row : row + NPOS, col : col + 128] = before
                columns[row : row + NPOS, col + 128 : col + DEPTH] = line


def place_kernel(arrived_ref, tall_ref, columns_ref, linear_ref, first_ref, wide):
    widen(tall_ref, wide)
    first_ref[...] = wide[0 : 3 * DEPTH, :]
    places = arrived_ref[:, :, REC:].reshape(NPOS, NPOS).astype(F32).T
    bz, bx, by = brick_rows((NPOS, NPOS), 0)

    def picker(sx, sy, sz):
        inside = (bx >= sx) & (by >= sy) & (bz >= sz)
        wanted = jnp.where(inside, (bx - sx) * 64 + (by - sy) * 8 + bz - sz, -2)
        return jnp.where(places == wanted.astype(F32), 1.0, 0.0).astype(BF16)

    for sx in range(2):
        for sy in range(2):
            pick = [picker(sx, sy, sz) for sz in range(2)]
            for vx in [3] if sx else range(4):
                for vy in [3] if sy else range(4):
                    at = (vx * 4 + vy) * LINE
                    source = arrived_ref[:, :, at : at + LINE].reshape(NPOS, LINE)
                    line = jnp.dot(pick[0], source, preferred_element_type=F32)
                    before = jnp.dot(pick[1], source[:, 256:], preferred_element_type=F32)
                    store_line(
                        columns_ref, line.astype(BF16), before.astype(BF16),
                        vx - 4 * sx, vy - 4 * sy, TAPS,
                    )
    linear_ref[...] = jnp.dot(columns_ref[...], wide[...], preferred_element_type=F32)


def layer_kernel(
    core_ref, columns_ref, linear_ref, first_ref, rim_ref, cotangent_ref,
    activation_ref, kept_ref, given_ref,
    front, linear, upstream, result, slopes, packed, left, turned_left,
):
    rz, rx, ry = brick_rows((NPOS, 64), 0)
    m = lax.broadcasted_iota(jnp.int32, (NPOS, 64), 1)

    def rim_picker(sy, sz):
        inside = (rx == 0) & (ry >= sy) & (rz >= sz)
        wanted = jnp.where(inside, (rz - sz) * 8 + ry - sy, -2)
        return jnp.where(m == wanted, 1.0, 0.0).astype(BF16)

    for sy in range(2):
        pick = [rim_picker(sy, sz) for sz in range(2)]
        for vy in [3] if sy else range(4):
            source = rim_ref[:, vy * LINE : (vy + 1) * LINE]
            line = jnp.dot(pick[0], source, preferred_element_type=F32)
            before = jnp.dot(pick[1], source[:, 256:], preferred_element_type=F32)
            store_line(front, line.astype(BF16), before.astype(BF16), -1, vy - 4 * sy, 3)
    half = 2 * NPOS
    linear[0:half, :] = linear_ref[0:half, :] + jnp.dot(
        front[...], first_ref[...], preferred_element_type=F32
    )
    linear[half:, :] = linear_ref[half:, :]
    front[...] += columns_ref[0:half, 0 : 3 * DEPTH]

    for tile in range(24):
        for x in range(4):
            upstream[x, tile] = cotangent_ref[x, :, tile * 128 : (tile + 1) * 128].astype(F32)
    for i in range(2):
        for j in range(2):
            for z in range(8):
                row = (i * 2 + j) * NPOS + z * 16
                value = linear[row : row + 16, :]
                sigma = 1.0 / (1.0 + jnp.exp(-value))
                active = value * sigma
                slope = sigma * (1.0 + value * (1.0 - sigma))
                incoming = []
                for tile in range(3):
                    lanes = slice(tile * 128, (tile + 1) * 128)
                    parts = []
                    for x in range(2):
                        at = (x * 2 + i, z * 3 + tile, pl.ds(j, 8, stride=2), slice(None))
                        parts.append(upstream[at])
                        result[at] = active[x * 8 : x * 8 + 8, lanes]
                    incoming.append(jnp.concatenate(parts, axis=0))
                incoming = jnp.concatenate(incoming, axis=1)
                change = (incoming * slope).astype(BF16)
                slopes[0, row : row + 16, :] = change[:, 0:C_OUT]
                slopes[1, row : row + 16, :] = change[:, C_OUT:]
    for tile in range(24):
        for x in range(4):
            activation_ref[x, :, tile * 128 : (tile + 1) * 128] = result[x, tile].astype(BF16)

    left[:, 64:128] = jnp.zeros((N_DP * 8, 64), F32)
    turned_left[:, N_DP * 8 :] = jnp.zeros((NPOS, NPOS - N_DP * 8), F32)
    for tap in range(TAPS):
        lanes = slice(tap * DEPTH, (tap + 1) * DEPTH)
        if tap < 3:
            turned = jnp.concatenate([front[:, lanes], columns_ref[half:, lanes]], axis=0).T
        else:
            turned = columns_ref[:, lanes].T
        product = [
            jnp.dot(turned[k * 128 : k * 128 + 384], slopes[k], preferred_element_type=F32)
            for k in range(2)
        ]
        block = product[0][32:320] + product[1][96:384]
        start = tap * 288
        while start < (tap + 1) * 288:
            d, row = divmod(start, SHARD)
            limit = KEEP if row < KEEP else SPLIT if row < SPLIT else SHARD
            stop = min((tap + 1) * 288, d * SHARD + limit)
            part = block[start - tap * 288 : stop - tap * 288]
            size = stop - start
            to = d * ROWS + row
            packed[to : to + size, :] = part[:, 0:128]
            if row < KEEP:
                packed[to + SHARD : to + SHARD + size, 0:64] = part[:, 128:C_OUT]
            elif row < SPLIT:
                to = d * 8 + row - KEEP
                left[to : to + size, 0:64] = part[:, 128:C_OUT]
            else:
                to = to + SHARD - SPLIT
                packed[to : to + size, 64:128] = part[:, 128:C_OUT]
            start = stop
    turned_left[:, 0 : N_DP * 8] = left[...].T
    core = core_ref[0]
    rows = N_DP * PIECE
    for chip in range(N_CHIP):
        for target, piece in ((kept_ref, 2 * chip + core), (given_ref, 2 * chip + 1 - core)):
            target[chip, 0:rows, :] = packed[pl.ds(piece, rows, stride=N_BRICK), :]
            target[chip, rows : rows + 1, :] = turned_left[pl.ds(piece, 1), :]
            target[chip, rows + 1 :, :] = jnp.zeros((TERM - rows - 1, 128), F32)


def chip_sum_kernel(terms_ref, sums_ref):
    total = terms_ref[0].astype(F32)
    for source in range(1, N_CHIP):
        total += terms_ref[source].astype(F32)
    last = N_DP * PIECE
    for d in range(N_DP):
        for row in range(PIECE):
            at = d * PIECE + row
            sums_ref[d, :, row * 128 : (row + 1) * 128] = total[at : at + 1]
        sums_ref[d, :, PIECE * 128 :] = jnp.concatenate(
            [total[last : last + 1, d * 8 : d * 8 + 8], jnp.zeros((1, 120), F32)], axis=1
        )


def scene_sum_kernel(sums_ref, copies_ref):
    total = sums_ref[0]
    for source in range(1, N_DP):
        total += sums_ref[source]
    for target in range(N_BRICK):
        copies_ref[target] = total


def unpack_kernel(pieces_ref, grad_ref, packed):
    for row in range(PIECE):
        packed[row * N_BRICK : (row + 1) * N_BRICK, :] = pieces_ref[
            :, 0, row * 128 : (row + 1) * 128
        ]
    grad_ref[0:128, :] = packed[0:SHARD, :].T
    grad_ref[128:C_OUT, 0:KEEP] = packed[SHARD : SHARD + KEEP, 0:64].T
    grad_ref[128:C_OUT, KEEP:SPLIT] = pieces_ref[:, 0, PIECE * 128 : PIECE * 128 + 128][:, 0:8]
    grad_ref[128:C_OUT, SPLIT:SHARD] = packed[SHARD : SHARD + KEEP, 64:128].T


def call(kernel, out, scratch=(), specs=(VMEM,), out_spec=VMEM, megabytes=8, flops=0):
    return pl.pallas_call(
        kernel,
        out_shape=out,
        in_specs=list(specs),
        out_specs=jax.tree.map(lambda _: out_spec, out),
        scratch_shapes=list(scratch),
        compiler_params=pltpu.CompilerParams(vmem_limit_bytes=megabytes * 1024 * 1024),
        cost_estimate=pl.CostEstimate(flops=flops, bytes_accessed=0, transcendentals=0) if flops else None,
    )


def spread(block, axis):
    return lax.all_to_all(block, axis, split_axis=0, concat_axis=0, tiled=True)


def body(records, positions, weight, cotangent):
    shape = jax.ShapeDtypeStruct
    sent = call(
        join_kernel,
        shape((N_BRICK, 2, REC + NPOS), BF16),
        [
            pltpu.VMEM((N_BRICK, 2, REC), BF16),
            pltpu.VMEM((N_BRICK, 2, NPOS), BF16),
            pltpu.VMEM((2, N_BRICK), jnp.int32),
            pltpu.VMEM((2 * N_BRICK, NPOS), F32),
            pltpu.SemaphoreType.DMA((2 * CHUNKS + 2,)),
        ],
        (HBM, HBM),
        HBM,
        61,
    )(records.reshape(N_BRICK, 2, REC), positions.reshape(N_BRICK, 2).T)
    arrived = spread(sent, BRICK)
    full_weight = lax.all_gather(weight.T, "dp", axis=0, tiled=False)
    tall = call(weight_kernel, shape((TAPS * 288, C_OUT), BF16))(full_weight)
    arrived, tall = lax.optimization_barrier((arrived, tall))
    rim = call(rim_kernel, shape((64, 4 * LINE), BF16))(arrived)
    rim = lax.ppermute(rim, BRICK, [(i, i + 1) for i in range(N_BRICK - 1)])
    columns, linear, first = call(
        place_kernel,
        (
            shape((4 * NPOS, TAPS * DEPTH), BF16),
            shape((4 * NPOS, LINE), F32),
            shape((3 * DEPTH, LINE), BF16),
        ),
        [pltpu.VMEM((TAPS * DEPTH, LINE), BF16)],
        (VMEM, VMEM),
        megabytes=16,
        flops=2 * 4 * NPOS * TAPS * DEPTH * LINE,
    )(arrived, tall)
    core = lax.axis_index("core").astype(jnp.int32).reshape(1)
    term = shape((N_CHIP, TERM, 128), F32)
    activation, kept, given = call(
        layer_kernel,
        (shape((4, 16, 8 * LINE), BF16), term, term),
        [
            pltpu.VMEM((2 * NPOS, 3 * DEPTH), BF16),
            pltpu.VMEM((4 * NPOS, LINE), F32),
            pltpu.VMEM((4, 24, 16, 128), F32),
            pltpu.VMEM((4, 24, 16, 128), F32),
            pltpu.VMEM((2, 4 * NPOS, C_OUT), BF16),
            pltpu.VMEM((TERM * N_BRICK, 128), F32),
            pltpu.VMEM((N_DP * 8, 128), F32),
            pltpu.VMEM((NPOS, NPOS), F32),
        ],
        (pl.BlockSpec(memory_space=pltpu.SMEM),) + (VMEM,) * 5,
        megabytes=16,
    )(core, columns, linear, first, rim, cotangent.reshape(4, 16, 8 * LINE))
    taken = lax.ppermute(given, "core", [(0, 1), (1, 0)])
    terms = spread((kept + taken).astype(BF16), ("x", "y"))
    sums = call(chip_sum_kernel, shape((N_DP, 1, WIDTH), F32))(terms)
    copies = call(scene_sum_kernel, shape((N_BRICK, 1, WIDTH), F32))(spread(sums, "dp"))
    grad = call(unpack_kernel, shape((C_OUT, SHARD), F32), [pltpu.VMEM((ROWS, 128), F32)])(
        spread(copies, BRICK)
    )
    return activation.reshape(cotangent.shape), grad.T


def solution(mesh):
    fine = jax.sharding.Mesh(mesh.devices.reshape(N_DP, 4, 8, 2), ("dp", "x", "y", "core"))
    placed = (
        P(("dp",) + BRICK, None, None, None),
        P(("dp",) + BRICK, None, None),
        P("dp", None),
        P("dp", BRICK, None, None),
    )
    return jax.shard_map(
        body,
        mesh=fine,
        in_specs=placed,
        out_specs=(P("dp", BRICK, None, None), P("dp", None)),
        check_vma=False,
    )
```

```python
import jax
import jax.numpy as jnp
from jax import lax
from jax.experimental import pallas as pl
from jax.experimental.pallas import tpu as pltpu
from jax.sharding import PartitionSpec as P

C_IN = 96
C_OUT = 192
REC = 6144
NPOS = 128
LINE = 384
DEPTH = 512
TAPS = 9
N_DP = 12
N_BRICK = 64
N_CHIP = 32
SHARD = 216
SPLIT = 112
KEEP = 104
PIECE = 5
TERM = 64
CHUNKS = 8
WIDTH = (PIECE + 1) * 128
ROWS = N_BRICK * PIECE
BRICK = ("x", "y", "core")
HBM = pl.BlockSpec(memory_space=pltpu.HBM)
VMEM = pl.BlockSpec(memory_space=pltpu.VMEM)
F32 = jnp.float32
BF16 = jnp.bfloat16


def join_kernel(records_ref, positions_ref, sent_ref, staged, tile, places, rows, sems):
    size = N_BRICK // CHUNKS
    coming = [pltpu.make_async_copy(positions_ref, places, sems.at[2 * CHUNKS])]
    going = []
    for part in range(CHUNKS):
        owners = pl.ds(part * size, size)
        coming.append(
            pltpu.make_async_copy(
                records_ref.at[owners], staged.at[owners], sems.at[part]
            )
        )
        going.append(
            pltpu.make_async_copy(
                staged.at[owners], sent_ref.at[owners, :, pl.ds(0, REC)], sems.at[CHUNKS + part]
            )
        )
    for copy in coming:
        copy.start()
    going.append(
        pltpu.make_async_copy(
            tile, sent_ref.at[:, :, pl.ds(REC, NPOS)], sems.at[2 * CHUNKS + 1]
        )
    )
    coming[0].wait()
    for slot in range(2):
        rows[pl.ds(slot, N_BRICK, stride=2), :] = jnp.broadcast_to(
            places[slot : slot + 1, :].astype(F32), (128, N_BRICK)
        ).T
    tile[...] = rows[...].astype(BF16).reshape(N_BRICK, 2, NPOS)
    going[CHUNKS].start()
    for part in range(CHUNKS):
        coming[1 + part].wait()
        going[part].start()
    for copy in going:
        copy.wait()


def brick_rows(shape, dim):
    q = lax.broadcasted_iota(jnp.int32, shape, dim)
    return q >> 4, (q >> 3) & 1, q & 7


def rim_kernel(arrived_ref, rim_ref):
    places = arrived_ref[:, :, REC:].reshape(NPOS, NPOS).astype(F32).T
    m = lax.broadcasted_iota(jnp.int32, (64, NPOS), 0)
    wanted = 64 + (m & 7) * 8 + (m >> 3)
    pick = jnp.where(places[:64] == wanted.astype(F32), 1.0, 0.0).astype(BF16)
    rim_ref[...] = jnp.dot(
        pick,
        arrived_ref[:, :, 12 * LINE : REC].reshape(NPOS, 4 * LINE),
        preferred_element_type=F32,
    ).astype(BF16)


def weight_kernel(weight_ref, tall_ref):
    for tap in range(TAPS):
        parts = []
        start = tap * 288
        while start < (tap + 1) * 288:
            d, row = divmod(start, SHARD)
            size = min((tap + 1) * 288, (d + 1) * SHARD) - start
            parts.append(weight_ref[d, :, row : row + size])
            start += size
        tall_ref[tap * 288 : (tap + 1) * 288, :] = jnp.concatenate(parts, axis=1).T


def widen(tall_ref, wide):
    for tap in range(TAPS):
        at = tap * DEPTH
        block = tall_ref[tap * 288 : (tap + 1) * 288, :]
        wide[at : at + 32, 0:C_OUT] = jnp.zeros((32, C_OUT), BF16)
        wide[at + 32 : at + 320, 0:C_OUT] = block
        wide[at + 320 : at + 512, 0:C_OUT] = jnp.zeros((192, C_OUT), BF16)
        wide[at : at + 224, C_OUT:] = jnp.zeros((224, C_OUT), BF16)
        wide[at + 224 : at + 512, C_OUT:] = block


def store_line(columns, line, before, ux, uy, width):
    for i in range(2 if width == TAPS else 1):
        for j in range(2):
            a = ux + 1 - 2 * i
            b = uy + 1 - 2 * j
            if 0 <= a <= 2 and 0 <= b <= 2:
                row = (i * 2 + j) * NPOS
                col = (a * 3 + b) * DEPTH
                columns[row : row + NPOS, col : col + 128] = before
                columns[row : row + NPOS, col + 128 : col + DEPTH] = line


def place_kernel(arrived_ref, tall_ref, columns_ref, linear_ref, first_ref, wide):
    widen(tall_ref, wide)
    first_ref[...] = wide[0 : 3 * DEPTH, :]
    places = arrived_ref[:, :, REC:].reshape(NPOS, NPOS).astype(F32).T
    bz, bx, by = brick_rows((NPOS, NPOS), 0)

    def picker(sx, sy, sz):
        inside = (bx >= sx) & (by >= sy) & (bz >= sz)
        wanted = jnp.where(inside, (bx - sx) * 64 + (by - sy) * 8 + bz - sz, -2)
        return jnp.where(places == wanted.astype(F32), 1.0, 0.0).astype(BF16)

    for sx in range(2):
        for sy in range(2):
            pick = jnp.concatenate([picker(sx, sy, sz) for sz in range(2)], axis=0)
            for vx in [3] if sx else range(4):
                for vy in [3] if sy else range(4):
                    at = (vx * 4 + vy) * LINE
                    source = arrived_ref[:, :, at : at + LINE].reshape(NPOS, LINE)
                    line = jnp.dot(pick[:NPOS], source[:, :256], preferred_element_type=F32)
                    ends = jnp.dot(pick, source[:, 256:], preferred_element_type=F32).astype(BF16)
                    line = jnp.concatenate([line.astype(BF16), ends[:NPOS]], axis=1)
                    store_line(columns_ref, line, ends[NPOS:], vx - 4 * sx, vy - 4 * sy, TAPS)
    linear_ref[...] = jnp.dot(columns_ref[...], wide[...], preferred_element_type=F32)


def layer_kernel(
    core_ref, columns_ref, linear_ref, first_ref, rim_ref, cotangent_ref,
    active_ref, kept_ref, given_ref,
    front, linear, upstream, slopes, packed, left, turned_left,
):
    rz, rx, ry = brick_rows((NPOS, 64), 0)
    m = lax.broadcasted_iota(jnp.int32, (NPOS, 64), 1)

    def rim_picker(sy, sz):
        inside = (rx == 0) & (ry >= sy) & (rz >= sz)
        wanted = jnp.where(inside, (rz - sz) * 8 + ry - sy, -2)
        return jnp.where(m == wanted, 1.0, 0.0).astype(BF16)

    for sy in range(2):
        pick = [rim_picker(sy, sz) for sz in range(2)]
        for vy in [3] if sy else range(4):
            source = rim_ref[:, vy * LINE : (vy + 1) * LINE]
            line = jnp.dot(pick[0], source, preferred_element_type=F32)
            before = jnp.dot(pick[1], source[:, 256:], preferred_element_type=F32)
            store_line(front, line.astype(BF16), before.astype(BF16), -1, vy - 4 * sy, 3)
    half = 2 * NPOS
    linear[0:half, :] = linear_ref[0:half, :] + jnp.dot(
        front[...], first_ref[...], preferred_element_type=F32
    )
    linear[half:, :] = linear_ref[half:, :]
    front[...] += columns_ref[0:half, 0 : 3 * DEPTH]

    for tile in range(24):
        for x in range(4):
            upstream[x, tile] = cotangent_ref[x, :, tile * 128 : (tile + 1) * 128].astype(F32)
    for i in range(2):
        for j in range(2):
            for z in range(8):
                row = (i * 2 + j) * NPOS + z * 16
                value = linear[row : row + 16, :]
                sigma = 1.0 / (1.0 + jnp.exp(-value))
                active_ref[row : row + 16, :] = (value * sigma).astype(BF16)
                slope = sigma * (1.0 + value * (1.0 - sigma))
                incoming = []
                for tile in range(3):
                    parts = [
                        upstream[x * 2 + i, z * 3 + tile, pl.ds(j, 8, stride=2), :]
                        for x in range(2)
                    ]
                    incoming.append(jnp.concatenate(parts, axis=0))
                incoming = jnp.concatenate(incoming, axis=1)
                change = (incoming * slope).astype(BF16)
                slopes[0, row : row + 16, :] = change[:, 0:C_OUT]
                slopes[1, row : row + 16, :] = change[:, C_OUT:]
    left[:, 64:128] = jnp.zeros((N_DP * 8, 64), F32)
    turned_left[:, N_DP * 8 :] = jnp.zeros((NPOS, NPOS - N_DP * 8), F32)
    for tap in range(TAPS):
        lanes = slice(tap * DEPTH, (tap + 1) * DEPTH)
        if tap < 3:
            turned = jnp.concatenate([front[:, lanes], columns_ref[half:, lanes]], axis=0).T
        else:
            turned = columns_ref[:, lanes].T
        product = [
            jnp.dot(turned[k * 128 : k * 128 + 384], slopes[k], preferred_element_type=F32)
            for k in range(2)
        ]
        block = product[0][32:320] + product[1][96:384]
        start = tap * 288
        while start < (tap + 1) * 288:
            d, row = divmod(start, SHARD)
            limit = KEEP if row < KEEP else SPLIT if row < SPLIT else SHARD
            stop = min((tap + 1) * 288, d * SHARD + limit)
            part = block[start - tap * 288 : stop - tap * 288]
            size = stop - start
            to = d * ROWS + row
            packed[to : to + size, :] = part[:, 0:128]
            if row < KEEP:
                packed[to + SHARD : to + SHARD + size, 0:64] = part[:, 128:C_OUT]
            elif row < SPLIT:
                to = d * 8 + row - KEEP
                left[to : to + size, 0:64] = part[:, 128:C_OUT]
            else:
                to = to + SHARD - SPLIT
                packed[to : to + size, 64:128] = part[:, 128:C_OUT]
            start = stop
    turned_left[:, 0 : N_DP * 8] = left[...].T
    core = core_ref[0]
    rows = N_DP * PIECE
    for chip in range(N_CHIP):
        for target, piece in ((kept_ref, 2 * chip + core), (given_ref, 2 * chip + 1 - core)):
            target[chip, 0:rows, :] = packed[pl.ds(piece, rows, stride=N_BRICK), :]
            target[chip, rows : rows + 1, :] = turned_left[pl.ds(piece, 1), :]
            target[chip, rows + 1 :, :] = jnp.zeros((TERM - rows - 1, 128), F32)


def finish_kernel(active_ref, activation_ref, result):
    for i in range(2):
        for j in range(2):
            for z in range(8):
                row = (i * 2 + j) * NPOS + z * 16
                active = active_ref[row : row + 16, :].astype(F32)
                for tile in range(3):
                    for x in range(2):
                        result[x * 2 + i, z * 3 + tile, pl.ds(j, 8, stride=2), :] = active[
                            x * 8 : x * 8 + 8, tile * 128 : (tile + 1) * 128
                        ]
    for tile in range(24):
        for x in range(4):
            activation_ref[x, :, tile * 128 : (tile + 1) * 128] = result[x, tile].astype(BF16)


def chip_sum_kernel(terms_ref, sums_ref):
    total = terms_ref[0].astype(F32)
    for source in range(1, N_CHIP):
        total += terms_ref[source].astype(F32)
    last = N_DP * PIECE
    for d in range(N_DP):
        for row in range(PIECE):
            at = d * PIECE + row
            sums_ref[d, :, row * 128 : (row + 1) * 128] = total[at : at + 1]
        sums_ref[d, :, PIECE * 128 :] = jnp.concatenate(
            [total[last : last + 1, d * 8 : d * 8 + 8], jnp.zeros((1, 120), F32)], axis=1
        )


def scene_sum_kernel(sums_ref, copies_ref):
    total = sums_ref[0]
    for source in range(1, N_DP):
        total += sums_ref[source]
    for target in range(N_BRICK):
        copies_ref[target] = total


def unpack_kernel(pieces_ref, grad_ref, packed):
    for row in range(PIECE):
        packed[row * N_BRICK : (row + 1) * N_BRICK, :] = pieces_ref[
            :, 0, row * 128 : (row + 1) * 128
        ]
    grad_ref[0:128, :] = packed[0:SHARD, :].T
    grad_ref[128:C_OUT, 0:KEEP] = packed[SHARD : SHARD + KEEP, 0:64].T
    grad_ref[128:C_OUT, KEEP:SPLIT] = pieces_ref[:, 0, PIECE * 128 : PIECE * 128 + 128][:, 0:8]
    grad_ref[128:C_OUT, SPLIT:SHARD] = packed[SHARD : SHARD + KEEP, 64:128].T


def call(kernel, out, scratch=(), specs=(VMEM,), out_spec=VMEM, megabytes=8, flops=0):
    return pl.pallas_call(
        kernel,
        out_shape=out,
        in_specs=list(specs),
        out_specs=jax.tree.map(lambda _: out_spec, out),
        scratch_shapes=list(scratch),
        compiler_params=pltpu.CompilerParams(vmem_limit_bytes=megabytes * 1024 * 1024),
        cost_estimate=pl.CostEstimate(flops=flops, bytes_accessed=0, transcendentals=0) if flops else None,
    )


def spread(block, axis):
    return lax.all_to_all(block, axis, split_axis=0, concat_axis=0, tiled=True)


def body(records, positions, weight, cotangent):
    shape = jax.ShapeDtypeStruct
    sent = call(
        join_kernel,
        shape((N_BRICK, 2, REC + NPOS), BF16),
        [
            pltpu.VMEM((N_BRICK, 2, REC), BF16),
            pltpu.VMEM((N_BRICK, 2, NPOS), BF16),
            pltpu.VMEM((2, N_BRICK), jnp.int32),
            pltpu.VMEM((2 * N_BRICK, NPOS), F32),
            pltpu.SemaphoreType.DMA((2 * CHUNKS + 2,)),
        ],
        (HBM, HBM),
        HBM,
        61,
    )(records.reshape(N_BRICK, 2, REC), positions.reshape(N_BRICK, 2).T)
    arrived = spread(sent, BRICK)
    full_weight = lax.all_gather(weight.T, "dp", axis=0, tiled=False)
    tall = call(weight_kernel, shape((TAPS * 288, C_OUT), BF16))(full_weight)
    arrived, tall = lax.optimization_barrier((arrived, tall))
    rim = call(rim_kernel, shape((64, 4 * LINE), BF16))(arrived)
    rim = lax.ppermute(rim, BRICK, [(i, i + 1) for i in range(N_BRICK - 1)])
    columns, linear, first = call(
        place_kernel,
        (
            shape((4 * NPOS, TAPS * DEPTH), BF16),
            shape((4 * NPOS, LINE), F32),
            shape((3 * DEPTH, LINE), BF16),
        ),
        [pltpu.VMEM((TAPS * DEPTH, LINE), BF16)],
        (VMEM, VMEM),
        megabytes=16,
        flops=2 * 4 * NPOS * TAPS * DEPTH * LINE,
    )(arrived, tall)
    core = lax.axis_index("core").astype(jnp.int32).reshape(1)
    term = shape((N_CHIP, TERM, 128), F32)
    active, kept, given = call(
        layer_kernel,
        (shape((4 * NPOS, LINE), BF16), term, term),
        [
            pltpu.VMEM((2 * NPOS, 3 * DEPTH), BF16),
            pltpu.VMEM((4 * NPOS, LINE), F32),
            pltpu.VMEM((4, 24, 16, 128), F32),
            pltpu.VMEM((2, 4 * NPOS, C_OUT), BF16),
            pltpu.VMEM((TERM * N_BRICK, 128), F32),
            pltpu.VMEM((N_DP * 8, 128), F32),
            pltpu.VMEM((NPOS, NPOS), F32),
        ],
        (pl.BlockSpec(memory_space=pltpu.SMEM),) + (VMEM,) * 5,
        megabytes=16,
    )(core, columns, linear, first, rim, cotangent.reshape(4, 16, 8 * LINE))
    taken = lax.ppermute(given, "core", [(0, 1), (1, 0)])
    activation = call(
        finish_kernel,
        shape((4, 16, 8 * LINE), BF16),
        [pltpu.VMEM((4, 24, 16, 128), F32)],
        flops=1024 * 1024,
    )(active)
    taken, activation = lax.optimization_barrier((taken, activation))
    terms = spread((kept + taken).astype(BF16), ("x", "y"))
    sums = call(chip_sum_kernel, shape((N_DP, 1, WIDTH), F32))(terms)
    copies = call(scene_sum_kernel, shape((N_BRICK, 1, WIDTH), F32))(spread(sums, "dp"))
    grad = call(unpack_kernel, shape((C_OUT, SHARD), F32), [pltpu.VMEM((ROWS, 128), F32)])(
        spread(copies, BRICK)
    )
    return activation.reshape(cotangent.shape), grad.T


def solution(mesh):
    fine = jax.sharding.Mesh(mesh.devices.reshape(N_DP, 4, 8, 2), ("dp", "x", "y", "core"))
    placed = (
        P(("dp",) + BRICK, None, None, None),
        P(("dp",) + BRICK, None, None),
        P("dp", None),
        P("dp", BRICK, None, None),
    )
    return jax.shard_map(
        body,
        mesh=fine,
        in_specs=placed,
        out_specs=(P("dp", BRICK, None, None), P("dp", None)),
        check_vma=False,
    )
```

```python
import jax
import jax.numpy as jnp
from jax import lax
from jax.experimental import pallas as pl
from jax.experimental.pallas import tpu as pltpu
from jax.sharding import PartitionSpec as P

C_IN = 96
C_OUT = 192
REC = 6144
NPOS = 128
LINE = 384
DEPTH = 512
TAPS = 9
N_DP = 12
N_BRICK = 64
N_CHIP = 32
SHARD = 216
SPLIT = 112
KEEP = 104
PIECE = 5
TERM = 64
CHUNKS = 8
WIDTH = (PIECE + 1) * 128
ROWS = N_BRICK * PIECE
BRICK = ("x", "y", "core")
HBM = pl.BlockSpec(memory_space=pltpu.HBM)
VMEM = pl.BlockSpec(memory_space=pltpu.VMEM)
F32 = jnp.float32
BF16 = jnp.bfloat16


def join_kernel(records_ref, positions_ref, sent_ref, staged, tile, places, rows, sems):
    size = N_BRICK // CHUNKS
    coming = [pltpu.make_async_copy(positions_ref, places, sems.at[2 * CHUNKS])]
    going = []
    for part in range(CHUNKS):
        owners = pl.ds(part * size, size)
        coming.append(
            pltpu.make_async_copy(
                records_ref.at[owners], staged.at[owners], sems.at[part]
            )
        )
        going.append(
            pltpu.make_async_copy(
                staged.at[owners], sent_ref.at[owners, :, pl.ds(0, REC)], sems.at[CHUNKS + part]
            )
        )
    for copy in coming:
        copy.start()
    going.append(
        pltpu.make_async_copy(
            tile, sent_ref.at[:, :, pl.ds(REC, NPOS)], sems.at[2 * CHUNKS + 1]
        )
    )
    coming[0].wait()
    for slot in range(2):
        rows[pl.ds(slot, N_BRICK, stride=2), :] = jnp.broadcast_to(
            places[slot : slot + 1, :].astype(F32), (128, N_BRICK)
        ).T
    tile[...] = rows[...].astype(BF16).reshape(N_BRICK, 2, NPOS)
    going[CHUNKS].start()
    for part in range(CHUNKS):
        coming[1 + part].wait()
        going[part].start()
    for copy in going:
        copy.wait()


def brick_rows(shape, dim):
    q = lax.broadcasted_iota(jnp.int32, shape, dim)
    return q >> 4, (q >> 3) & 1, q & 7


def rim_kernel(arrived_ref, rim_ref):
    places = arrived_ref[:, :, REC:].reshape(NPOS, NPOS).astype(F32).T
    m = lax.broadcasted_iota(jnp.int32, (64, NPOS), 0)
    wanted = 64 + (m & 7) * 8 + (m >> 3)
    pick = jnp.where(places[:64] == wanted.astype(F32), 1.0, 0.0).astype(BF16)
    rim_ref[...] = jnp.dot(
        pick,
        arrived_ref[:, :, 12 * LINE : REC].reshape(NPOS, 4 * LINE),
        preferred_element_type=F32,
    ).astype(BF16)


def weight_kernel(weight_ref, tall_ref):
    for tap in range(TAPS):
        parts = []
        start = tap * 288
        while start < (tap + 1) * 288:
            d, row = divmod(start, SHARD)
            size = min((tap + 1) * 288, (d + 1) * SHARD) - start
            parts.append(weight_ref[d, :, row : row + size])
            start += size
        tall_ref[tap * 288 : (tap + 1) * 288, :] = jnp.concatenate(parts, axis=1).T


def widen(tall_ref, wide):
    for tap in range(TAPS):
        at = tap * DEPTH
        block = tall_ref[tap * 288 : (tap + 1) * 288, :]
        wide[at : at + 32, 0:C_OUT] = jnp.zeros((32, C_OUT), BF16)
        wide[at + 32 : at + 320, 0:C_OUT] = block
        wide[at + 320 : at + 512, 0:C_OUT] = jnp.zeros((192, C_OUT), BF16)
        wide[at : at + 224, C_OUT:] = jnp.zeros((224, C_OUT), BF16)
        wide[at + 224 : at + 512, C_OUT:] = block


def store_line(columns, line, before, ux, uy, width):
    for i in range(2 if width == TAPS else 1):
        for j in range(2):
            a = ux + 1 - 2 * i
            b = uy + 1 - 2 * j
            if 0 <= a <= 2 and 0 <= b <= 2:
                row = (i * 2 + j) * NPOS
                col = (a * 3 + b) * DEPTH
                columns[row : row + NPOS, col : col + 128] = before
                columns[row : row + NPOS, col + 128 : col + DEPTH] = line


def place_kernel(arrived_ref, tall_ref, columns_ref, linear_ref, first_ref, wide):
    widen(tall_ref, wide)
    first_ref[...] = wide[0 : 3 * DEPTH, :]
    places = arrived_ref[:, :, REC:].reshape(NPOS, NPOS).astype(F32).T
    bz, bx, by = brick_rows((NPOS, NPOS), 0)

    def picker(sx, sy, sz):
        inside = (bx >= sx) & (by >= sy) & (bz >= sz)
        wanted = jnp.where(inside, (bx - sx) * 64 + (by - sy) * 8 + bz - sz, -2)
        return jnp.where(places == wanted.astype(F32), 1.0, 0.0).astype(BF16)

    for sx in range(2):
        for sy in range(2):
            pick = jnp.concatenate([picker(sx, sy, sz) for sz in range(2)], axis=0)
            for vx in [3] if sx else range(4):
                for vy in [3] if sy else range(4):
                    at = (vx * 4 + vy) * LINE
                    source = arrived_ref[:, :, at : at + LINE].reshape(NPOS, LINE)
                    line = jnp.dot(pick[:NPOS], source[:, :256], preferred_element_type=F32)
                    ends = jnp.dot(pick, source[:, 256:], preferred_element_type=F32).astype(BF16)
                    line = jnp.concatenate([line.astype(BF16), ends[:NPOS]], axis=1)
                    store_line(columns_ref, line, ends[NPOS:], vx - 4 * sx, vy - 4 * sy, TAPS)
    linear_ref[...] = jnp.dot(columns_ref[...], wide[...], preferred_element_type=F32)


def layer_kernel(
    core_ref, columns_ref, linear_ref, first_ref, rim_ref, cotangent_ref,
    active_ref, kept_ref, given_ref,
    front, linear, upstream, slopes, packed, left, turned_left,
):
    rz, rx, ry = brick_rows((NPOS, 64), 0)
    m = lax.broadcasted_iota(jnp.int32, (NPOS, 64), 1)

    def rim_picker(sy, sz):
        inside = (rx == 0) & (ry >= sy) & (rz >= sz)
        wanted = jnp.where(inside, (rz - sz) * 8 + ry - sy, -2)
        return jnp.where(m == wanted, 1.0, 0.0).astype(BF16)

    for sy in range(2):
        pick = [rim_picker(sy, sz) for sz in range(2)]
        for vy in [3] if sy else range(4):
            source = rim_ref[:, vy * LINE : (vy + 1) * LINE]
            line = jnp.dot(pick[0], source, preferred_element_type=F32)
            before = jnp.dot(pick[1], source[:, 256:], preferred_element_type=F32)
            store_line(front, line.astype(BF16), before.astype(BF16), -1, vy - 4 * sy, 3)
    half = 2 * NPOS
    linear[0:half, :] = linear_ref[0:half, :] + jnp.dot(
        front[...], first_ref[...], preferred_element_type=F32
    )
    linear[half:, :] = linear_ref[half:, :]
    front[...] += columns_ref[0:half, 0 : 3 * DEPTH]

    for tile in range(24):
        for x in range(4):
            upstream[x, tile] = cotangent_ref[x, :, tile * 128 : (tile + 1) * 128].astype(F32)
    for i in range(2):
        for j in range(2):
            for z in range(8):
                row = (i * 2 + j) * NPOS + z * 16
                value = linear[row : row + 16, :]
                sigma = 1.0 / (1.0 + jnp.exp(-value))
                active_ref[row : row + 16, :] = (value * sigma).astype(BF16)
                slope = sigma * (1.0 + value * (1.0 - sigma))
                incoming = []
                for tile in range(3):
                    parts = [
                        upstream[x * 2 + i, z * 3 + tile, pl.ds(j, 8, stride=2), :]
                        for x in range(2)
                    ]
                    incoming.append(jnp.concatenate(parts, axis=0))
                incoming = jnp.concatenate(incoming, axis=1)
                change = (incoming * slope).astype(BF16)
                slopes[0, row : row + 16, :] = change[:, 0:C_OUT]
                slopes[1, row : row + 16, :] = change[:, C_OUT:]
    left[:, 64:128] = jnp.zeros((N_DP * 8, 64), F32)
    turned_left[:, N_DP * 8 :] = jnp.zeros((NPOS, NPOS - N_DP * 8), F32)
    for tap in range(TAPS):
        lanes = slice(tap * DEPTH, (tap + 1) * DEPTH)
        if tap < 3:
            turned = jnp.concatenate([front[:, lanes], columns_ref[half:, lanes]], axis=0).T
        else:
            turned = columns_ref[:, lanes].T
        product = [
            jnp.dot(turned[k * 128 : k * 128 + 384], slopes[k], preferred_element_type=F32)
            for k in range(2)
        ]
        block = product[0][32:320] + product[1][96:384]
        start = tap * 288
        while start < (tap + 1) * 288:
            d, row = divmod(start, SHARD)
            limit = KEEP if row < KEEP else SPLIT if row < SPLIT else SHARD
            stop = min((tap + 1) * 288, d * SHARD + limit)
            part = block[start - tap * 288 : stop - tap * 288]
            size = stop - start
            to = d * ROWS + row
            packed[to : to + size, :] = part[:, 0:128]
            if row < KEEP:
                packed[to + SHARD : to + SHARD + size, 0:64] = part[:, 128:C_OUT]
            elif row < SPLIT:
                to = d * 8 + row - KEEP
                left[to : to + size, 0:64] = part[:, 128:C_OUT]
            else:
                to = to + SHARD - SPLIT
                packed[to : to + size, 64:128] = part[:, 128:C_OUT]
            start = stop
    turned_left[:, 0 : N_DP * 8] = left[...].T
    core = core_ref[0]
    rows = N_DP * PIECE
    for chip in range(N_CHIP):
        for target, piece in ((kept_ref, 2 * chip + core), (given_ref, 2 * chip + 1 - core)):
            target[chip, 0:rows, :] = packed[pl.ds(piece, rows, stride=N_BRICK), :]
            target[chip, rows : rows + 1, :] = turned_left[pl.ds(piece, 1), :]
            target[chip, rows + 1 :, :] = jnp.zeros((TERM - rows - 1, 128), F32)


def finish_kernel(active_ref, activation_ref, result):
    for i in range(2):
        for j in range(2):
            for z in range(8):
                row = (i * 2 + j) * NPOS + z * 16
                active = active_ref[row : row + 16, :].astype(F32)
                for tile in range(3):
                    for x in range(2):
                        result[x * 2 + i, z * 3 + tile, pl.ds(j, 8, stride=2), :] = active[
                            x * 8 : x * 8 + 8, tile * 128 : (tile + 1) * 128
                        ]
    for tile in range(24):
        for x in range(4):
            activation_ref[x, :, tile * 128 : (tile + 1) * 128] = result[x, tile].astype(BF16)


def chip_sum_kernel(terms_ref, sums_ref):
    total = terms_ref[0].astype(F32)
    for source in range(1, N_CHIP):
        total += terms_ref[source].astype(F32)
    last = N_DP * PIECE
    for d in range(N_DP):
        ends = total[last : last + 1, d * 8 : d * 8 + 8]
        ends = jnp.concatenate([ends, jnp.zeros((1, 120), F32)], axis=1)
        for core in range(2):
            for row in range(PIECE):
                at = d * PIECE + row
                sums_ref[2 * d + core, :, row * 128 : (row + 1) * 128] = total[at : at + 1]
            sums_ref[2 * d + core, :, PIECE * 128 :] = ends


def scene_sum_kernel(sums_ref, copies_ref):
    for core in range(2):
        total = sums_ref[core]
        for source in range(1, N_DP):
            total += sums_ref[2 * source + core]
        for target in range(N_CHIP):
            copies_ref[target, :, core * WIDTH : (core + 1) * WIDTH] = total


def unpack_kernel(pieces_ref, grad_ref, packed):
    for core in range(2):
        for row in range(PIECE + 1):
            at = core * WIDTH + row * 128
            packed[pl.ds(row * N_BRICK + core, N_CHIP, stride=2), :] = pieces_ref[
                :, 0, at : at + 128
            ]
    grad_ref[0:128, :] = packed[0:SHARD, :].T
    grad_ref[128:C_OUT, 0:KEEP] = packed[SHARD : SHARD + KEEP, 0:64].T
    grad_ref[128:C_OUT, KEEP:SPLIT] = packed[ROWS : ROWS + N_BRICK, 0:8]
    grad_ref[128:C_OUT, SPLIT:SHARD] = packed[SHARD : SHARD + KEEP, 64:128].T


def call(kernel, out, scratch=(), specs=(VMEM,), out_spec=VMEM, megabytes=8, flops=0):
    return pl.pallas_call(
        kernel,
        out_shape=out,
        in_specs=list(specs),
        out_specs=jax.tree.map(lambda _: out_spec, out),
        scratch_shapes=list(scratch),
        compiler_params=pltpu.CompilerParams(vmem_limit_bytes=megabytes * 1024 * 1024),
        cost_estimate=pl.CostEstimate(flops=flops, bytes_accessed=0, transcendentals=0) if flops else None,
    )


def spread(block, axis):
    return lax.all_to_all(block, axis, split_axis=0, concat_axis=0, tiled=True)


def body(records, positions, weight, cotangent):
    shape = jax.ShapeDtypeStruct
    sent = call(
        join_kernel,
        shape((N_BRICK, 2, REC + NPOS), BF16),
        [
            pltpu.VMEM((N_BRICK, 2, REC), BF16),
            pltpu.VMEM((N_BRICK, 2, NPOS), BF16),
            pltpu.VMEM((2, N_BRICK), jnp.int32),
            pltpu.VMEM((2 * N_BRICK, NPOS), F32),
            pltpu.SemaphoreType.DMA((2 * CHUNKS + 2,)),
        ],
        (HBM, HBM),
        HBM,
        61,
    )(records.reshape(N_BRICK, 2, REC), positions.reshape(N_BRICK, 2).T)
    arrived = spread(sent, BRICK)
    full_weight = lax.all_gather(weight.T, "dp", axis=0, tiled=False)
    tall = call(weight_kernel, shape((TAPS * 288, C_OUT), BF16))(full_weight)
    arrived, tall = lax.optimization_barrier((arrived, tall))
    rim = call(rim_kernel, shape((64, 4 * LINE), BF16))(arrived)
    rim = lax.ppermute(rim, BRICK, [(i, i + 1) for i in range(N_BRICK - 1)])
    columns, linear, first = call(
        place_kernel,
        (
            shape((4 * NPOS, TAPS * DEPTH), BF16),
            shape((4 * NPOS, LINE), F32),
            shape((3 * DEPTH, LINE), BF16),
        ),
        [pltpu.VMEM((TAPS * DEPTH, LINE), BF16)],
        (VMEM, VMEM),
        megabytes=16,
        flops=2 * 4 * NPOS * TAPS * DEPTH * LINE,
    )(arrived, tall)
    core = lax.axis_index("core").astype(jnp.int32).reshape(1)
    term = shape((N_CHIP, TERM, 128), F32)
    active, kept, given = call(
        layer_kernel,
        (shape((4 * NPOS, LINE), BF16), term, term),
        [
            pltpu.VMEM((2 * NPOS, 3 * DEPTH), BF16),
            pltpu.VMEM((4 * NPOS, LINE), F32),
            pltpu.VMEM((4, 24, 16, 128), F32),
            pltpu.VMEM((2, 4 * NPOS, C_OUT), BF16),
            pltpu.VMEM((TERM * N_BRICK, 128), F32),
            pltpu.VMEM((N_DP * 8, 128), F32),
            pltpu.VMEM((NPOS, NPOS), F32),
        ],
        (pl.BlockSpec(memory_space=pltpu.SMEM),) + (VMEM,) * 5,
        megabytes=16,
    )(core, columns, linear, first, rim, cotangent.reshape(4, 16, 8 * LINE))
    taken = lax.ppermute(given, "core", [(0, 1), (1, 0)])
    activation = call(
        finish_kernel,
        shape((4, 16, 8 * LINE), BF16),
        [pltpu.VMEM((4, 24, 16, 128), F32)],
        flops=1024 * 1024,
    )(active)
    taken, activation = lax.optimization_barrier((taken, activation))
    terms = spread((kept + taken).astype(BF16), ("x", "y"))
    sums = call(chip_sum_kernel, shape((2 * N_DP, 1, WIDTH), F32))(terms)
    sums = spread(sums, ("dp", "core"))
    copies = call(scene_sum_kernel, shape((N_CHIP, 1, 2 * WIDTH), F32))(sums)
    grad = call(
        unpack_kernel,
        shape((C_OUT, SHARD), F32),
        [pltpu.VMEM((ROWS + N_BRICK, 128), F32)],
    )(spread(copies, ("x", "y")))
    return activation.reshape(cotangent.shape), grad.T


def solution(mesh):
    fine = jax.sharding.Mesh(mesh.devices.reshape(N_DP, 4, 8, 2), ("dp", "x", "y", "core"))
    placed = (
        P(("dp",) + BRICK, None, None, None),
        P(("dp",) + BRICK, None, None),
        P("dp", None),
        P("dp", BRICK, None, None),
    )
    return jax.shard_map(
        body,
        mesh=fine,
        in_specs=placed,
        out_specs=(P("dp", BRICK, None, None), P("dp", None)),
        check_vma=False,
    )
```

```python
import jax
import jax.numpy as jnp
from jax import lax
from jax.experimental import pallas as pl
from jax.experimental.pallas import tpu as pltpu
from jax.sharding import PartitionSpec as P

C_IN = 96
C_OUT = 192
REC = 6144
NPOS = 128
LINE = 384
DEPTH = 512
TAPS = 9
N_DP = 12
N_BRICK = 64
N_CHIP = 32
SHARD = 216
SPLIT = 112
KEEP = 104
PIECE = 5
TERM = 64
CHUNKS = 4
WIDTH = (PIECE + 1) * 128
ROWS = N_BRICK * PIECE
BRICK = ("x", "y", "core")
HBM = pl.BlockSpec(memory_space=pltpu.HBM)
VMEM = pl.BlockSpec(memory_space=pltpu.VMEM)
F32 = jnp.float32
BF16 = jnp.bfloat16


def join_kernel(records_ref, positions_ref, sent_ref, staged, tile, places, rows, sems):
    size = N_BRICK // CHUNKS
    coming = [pltpu.make_async_copy(positions_ref, places, sems.at[2 * CHUNKS])]
    going = []
    for part in range(CHUNKS):
        owners = pl.ds(part * size, size)
        coming.append(
            pltpu.make_async_copy(
                records_ref.at[owners], staged.at[owners], sems.at[part]
            )
        )
        going.append(
            pltpu.make_async_copy(
                staged.at[owners], sent_ref.at[owners, :, pl.ds(0, REC)], sems.at[CHUNKS + part]
            )
        )
    for copy in coming:
        copy.start()
    going.append(
        pltpu.make_async_copy(
            tile, sent_ref.at[:, :, pl.ds(REC, NPOS)], sems.at[2 * CHUNKS + 1]
        )
    )
    coming[0].wait()
    for slot in range(2):
        rows[pl.ds(slot, N_BRICK, stride=2), :] = jnp.broadcast_to(
            places[slot : slot + 1, :].astype(F32), (128, N_BRICK)
        ).T
    tile[...] = rows[...].astype(BF16).reshape(N_BRICK, 2, NPOS)
    going[CHUNKS].start()
    for part in range(CHUNKS):
        coming[1 + part].wait()
        going[part].start()
    for copy in going:
        copy.wait()


def brick_rows(shape, dim):
    q = lax.broadcasted_iota(jnp.int32, shape, dim)
    return q >> 4, (q >> 3) & 1, q & 7


def rim_kernel(arrived_ref, rim_ref):
    places = arrived_ref[:, :, REC:].reshape(NPOS, NPOS).astype(F32).T
    m = lax.broadcasted_iota(jnp.int32, (64, NPOS), 0)
    wanted = 64 + (m & 7) * 8 + (m >> 3)
    pick = jnp.where(places[:64] == wanted.astype(F32), 1.0, 0.0).astype(BF16)
    rim_ref[...] = jnp.dot(
        pick,
        arrived_ref[:, :, 12 * LINE : REC].reshape(NPOS, 4 * LINE),
        preferred_element_type=F32,
    ).astype(BF16)


def weight_kernel(weight_ref, tall_ref):
    for tap in range(TAPS):
        parts = []
        start = tap * 288
        while start < (tap + 1) * 288:
            d, row = divmod(start, SHARD)
            size = min((tap + 1) * 288, (d + 1) * SHARD) - start
            parts.append(weight_ref[d, :, row : row + size])
            start += size
        tall_ref[tap * 288 : (tap + 1) * 288, :] = jnp.concatenate(parts, axis=1).T


def widen(tall_ref, wide):
    for tap in range(TAPS):
        at = tap * DEPTH
        block = tall_ref[tap * 288 : (tap + 1) * 288, :]
        wide[at : at + 32, 0:C_OUT] = jnp.zeros((32, C_OUT), BF16)
        wide[at + 32 : at + 320, 0:C_OUT] = block
        wide[at + 320 : at + 512, 0:C_OUT] = jnp.zeros((192, C_OUT), BF16)
        wide[at : at + 224, C_OUT:] = jnp.zeros((224, C_OUT), BF16)
        wide[at + 224 : at + 512, C_OUT:] = block


def store_line(columns, line, before, ux, uy, width):
    for i in range(2 if width == TAPS else 1):
        for j in range(2):
            a = ux + 1 - 2 * i
            b = uy + 1 - 2 * j
            if 0 <= a <= 2 and 0 <= b <= 2:
                row = (i * 2 + j) * NPOS
                col = (a * 3 + b) * DEPTH
                columns[row : row + NPOS, col : col + 128] = before
                columns[row : row + NPOS, col + 128 : col + DEPTH] = line


def place_kernel(arrived_ref, tall_ref, columns_ref, linear_ref, first_ref, wide):
    widen(tall_ref, wide)
    first_ref[...] = wide[0 : 3 * DEPTH, :]
    places = arrived_ref[:, :, REC:].reshape(NPOS, NPOS).astype(F32).T
    bz, bx, by = brick_rows((NPOS, NPOS), 0)

    def picker(sx, sy, sz):
        inside = (bx >= sx) & (by >= sy) & (bz >= sz)
        wanted = jnp.where(inside, (bx - sx) * 64 + (by - sy) * 8 + bz - sz, -2)
        return jnp.where(places == wanted.astype(F32), 1.0, 0.0).astype(BF16)

    for sx in range(2):
        for sy in range(2):
            pick = jnp.concatenate([picker(sx, sy, sz) for sz in range(2)], axis=0)
            for vx in [3] if sx else range(4):
                for vy in [3] if sy else range(4):
                    at = (vx * 4 + vy) * LINE
                    source = arrived_ref[:, :, at : at + LINE].reshape(NPOS, LINE)
                    line = jnp.dot(pick[:NPOS], source[:, :256], preferred_element_type=F32)
                    ends = jnp.dot(pick, source[:, 256:], preferred_element_type=F32).astype(BF16)
                    line = jnp.concatenate([line.astype(BF16), ends[:NPOS]], axis=1)
                    store_line(columns_ref, line, ends[NPOS:], vx - 4 * sx, vy - 4 * sy, TAPS)
    linear_ref[...] = jnp.dot(columns_ref[...], wide[...], preferred_element_type=F32)


def layer_kernel(
    core_ref, columns_ref, linear_ref, first_ref, rim_ref, cotangent_ref,
    active_ref, kept_ref, given_ref,
    front, linear, upstream, slopes, packed, left, turned_left,
):
    rz, rx, ry = brick_rows((NPOS, 64), 0)
    m = lax.broadcasted_iota(jnp.int32, (NPOS, 64), 1)

    def rim_picker(sy, sz):
        inside = (rx == 0) & (ry >= sy) & (rz >= sz)
        wanted = jnp.where(inside, (rz - sz) * 8 + ry - sy, -2)
        return jnp.where(m == wanted, 1.0, 0.0).astype(BF16)

    for sy in range(2):
        pick = [rim_picker(sy, sz) for sz in range(2)]
        for vy in [3] if sy else range(4):
            source = rim_ref[:, vy * LINE : (vy + 1) * LINE]
            line = jnp.dot(pick[0], source, preferred_element_type=F32)
            before = jnp.dot(pick[1], source[:, 256:], preferred_element_type=F32)
            store_line(front, line.astype(BF16), before.astype(BF16), -1, vy - 4 * sy, 3)
    half = 2 * NPOS
    linear[0:half, :] = linear_ref[0:half, :] + jnp.dot(
        front[...], first_ref[...], preferred_element_type=F32
    )
    linear[half:, :] = linear_ref[half:, :]
    front[...] += columns_ref[0:half, 0 : 3 * DEPTH]

    for tile in range(24):
        for x in range(4):
            upstream[x, tile] = cotangent_ref[x, :, tile * 128 : (tile + 1) * 128].astype(F32)
    for i in range(2):
        for j in range(2):
            for z in range(8):
                row = (i * 2 + j) * NPOS + z * 16
                value = linear[row : row + 16, :]
                sigma = 1.0 / (1.0 + jnp.exp(-value))
                active_ref[row : row + 16, :] = (value * sigma).astype(BF16)
                slope = sigma * (1.0 + value * (1.0 - sigma))
                incoming = []
                for tile in range(3):
                    parts = [
                        upstream[x * 2 + i, z * 3 + tile, pl.ds(j, 8, stride=2), :]
                        for x in range(2)
                    ]
                    incoming.append(jnp.concatenate(parts, axis=0))
                incoming = jnp.concatenate(incoming, axis=1)
                change = (incoming * slope).astype(BF16)
                slopes[0, row : row + 16, :] = change[:, 0:C_OUT]
                slopes[1, row : row + 16, :] = change[:, C_OUT:]
    left[:, 64:128] = jnp.zeros((N_DP * 8, 64), F32)
    turned_left[:, N_DP * 8 :] = jnp.zeros((NPOS, NPOS - N_DP * 8), F32)
    for tap in range(TAPS):
        lanes = slice(tap * DEPTH, (tap + 1) * DEPTH)
        if tap < 3:
            turned = jnp.concatenate([front[:, lanes], columns_ref[half:, lanes]], axis=0).T
        else:
            turned = columns_ref[:, lanes].T
        product = [
            jnp.dot(turned[k * 128 : k * 128 + 384], slopes[k], preferred_element_type=F32)
            for k in range(2)
        ]
        block = product[0][32:320] + product[1][96:384]
        start = tap * 288
        while start < (tap + 1) * 288:
            d, row = divmod(start, SHARD)
            limit = KEEP if row < KEEP else SPLIT if row < SPLIT else SHARD
            stop = min((tap + 1) * 288, d * SHARD + limit)
            part = block[start - tap * 288 : stop - tap * 288]
            size = stop - start
            to = d * ROWS + row
            packed[to : to + size, :] = part[:, 0:128]
            if row < KEEP:
                packed[to + SHARD : to + SHARD + size, 0:64] = part[:, 128:C_OUT]
            elif row < SPLIT:
                to = d * 8 + row - KEEP
                left[to : to + size, 0:64] = part[:, 128:C_OUT]
            else:
                to = to + SHARD - SPLIT
                packed[to : to + size, 64:128] = part[:, 128:C_OUT]
            start = stop
    turned_left[:, 0 : N_DP * 8] = left[...].T
    core = core_ref[0]
    rows = N_DP * PIECE
    for chip in range(N_CHIP):
        for target, piece in ((kept_ref, 2 * chip + core), (given_ref, 2 * chip + 1 - core)):
            target[chip, 0:rows, :] = packed[pl.ds(piece, rows, stride=N_BRICK), :]
            target[chip, rows : rows + 1, :] = turned_left[pl.ds(piece, 1), :]
            target[chip, rows + 1 :, :] = jnp.zeros((TERM - rows - 1, 128), F32)


def finish_kernel(active_ref, activation_ref, result):
    for i in range(2):
        for j in range(2):
            for z in range(8):
                row = (i * 2 + j) * NPOS + z * 16
                active = active_ref[row : row + 16, :].astype(F32)
                for tile in range(3):
                    for x in range(2):
                        result[x * 2 + i, z * 3 + tile, pl.ds(j, 8, stride=2), :] = active[
                            x * 8 : x * 8 + 8, tile * 128 : (tile + 1) * 128
                        ]
    for tile in range(24):
        for x in range(4):
            activation_ref[x, :, tile * 128 : (tile + 1) * 128] = result[x, tile].astype(BF16)


def chip_sum_kernel(terms_ref, sums_ref):
    total = terms_ref[0].astype(F32)
    for source in range(1, N_CHIP):
        total += terms_ref[source].astype(F32)
    last = N_DP * PIECE
    for d in range(N_DP):
        for row in range(PIECE):
            at = d * PIECE + row
            sums_ref[d, :, row * 128 : (row + 1) * 128] = total[at : at + 1]
        sums_ref[d, :, PIECE * 128 :] = jnp.concatenate(
            [total[last : last + 1, d * 8 : d * 8 + 8], jnp.zeros((1, 120), F32)], axis=1
        )


def scene_sum_kernel(sums_ref, copies_ref):
    total = sums_ref[0]
    for source in range(1, N_DP):
        total += sums_ref[source]
    for target in range(N_BRICK):
        copies_ref[target] = total


def unpack_kernel(pieces_ref, grad_ref, packed):
    for row in range(PIECE):
        packed[row * N_BRICK : (row + 1) * N_BRICK, :] = pieces_ref[
            :, 0, row * 128 : (row + 1) * 128
        ]
    grad_ref[0:128, :] = packed[0:SHARD, :].T
    grad_ref[128:C_OUT, 0:KEEP] = packed[SHARD : SHARD + KEEP, 0:64].T
    grad_ref[128:C_OUT, KEEP:SPLIT] = pieces_ref[:, 0, PIECE * 128 : PIECE * 128 + 128][:, 0:8]
    grad_ref[128:C_OUT, SPLIT:SHARD] = packed[SHARD : SHARD + KEEP, 64:128].T


def call(kernel, out, scratch=(), specs=(VMEM,), out_spec=VMEM, megabytes=8, flops=0):
    return pl.pallas_call(
        kernel,
        out_shape=out,
        in_specs=list(specs),
        out_specs=jax.tree.map(lambda _: out_spec, out),
        scratch_shapes=list(scratch),
        compiler_params=pltpu.CompilerParams(vmem_limit_bytes=megabytes * 1024 * 1024),
        cost_estimate=pl.CostEstimate(flops=flops, bytes_accessed=0, transcendentals=0) if flops else None,
    )


def spread(block, axis):
    return lax.all_to_all(block, axis, split_axis=0, concat_axis=0, tiled=True)


def body(records, positions, weight, cotangent):
    shape = jax.ShapeDtypeStruct
    sent = call(
        join_kernel,
        shape((N_BRICK, 2, REC + NPOS), BF16),
        [
            pltpu.VMEM((N_BRICK, 2, REC), BF16),
            pltpu.VMEM((N_BRICK, 2, NPOS), BF16),
            pltpu.VMEM((2, N_BRICK), jnp.int32),
            pltpu.VMEM((2 * N_BRICK, NPOS), F32),
            pltpu.SemaphoreType.DMA((2 * CHUNKS + 2,)),
        ],
        (HBM, HBM),
        HBM,
        61,
    )(records.reshape(N_BRICK, 2, REC), positions.reshape(N_BRICK, 2).T)
    arrived = spread(sent, BRICK)
    full_weight = lax.all_gather(weight.T, "dp", axis=0, tiled=False)
    tall = call(weight_kernel, shape((TAPS * 288, C_OUT), BF16))(full_weight)
    arrived, tall = lax.optimization_barrier((arrived, tall))
    rim = call(rim_kernel, shape((64, 4 * LINE), BF16))(arrived)
    rim = lax.ppermute(rim, BRICK, [(i, i + 1) for i in range(N_BRICK - 1)])
    columns, linear, first = call(
        place_kernel,
        (
            shape((4 * NPOS, TAPS * DEPTH), BF16),
            shape((4 * NPOS, LINE), F32),
            shape((3 * DEPTH, LINE), BF16),
        ),
        [pltpu.VMEM((TAPS * DEPTH, LINE), BF16)],
        (VMEM, VMEM),
        megabytes=16,
        flops=2 * 4 * NPOS * TAPS * DEPTH * LINE,
    )(arrived, tall)
    core = lax.axis_index("core").astype(jnp.int32).reshape(1)
    term = shape((N_CHIP, TERM, 128), F32)
    active, kept, given = call(
        layer_kernel,
        (shape((4 * NPOS, LINE), BF16), term, term),
        [
            pltpu.VMEM((2 * NPOS, 3 * DEPTH), BF16),
            pltpu.VMEM((4 * NPOS, LINE), F32),
            pltpu.VMEM((4, 24, 16, 128), F32),
            pltpu.VMEM((2, 4 * NPOS, C_OUT), BF16),
            pltpu.VMEM((TERM * N_BRICK, 128), F32),
            pltpu.VMEM((N_DP * 8, 128), F32),
            pltpu.VMEM((NPOS, NPOS), F32),
        ],
        (pl.BlockSpec(memory_space=pltpu.SMEM),) + (VMEM,) * 5,
        megabytes=16,
    )(core, columns, linear, first, rim, cotangent.reshape(4, 16, 8 * LINE))
    taken = lax.ppermute(given, "core", [(0, 1), (1, 0)])
    activation = call(
        finish_kernel,
        shape((4, 16, 8 * LINE), BF16),
        [pltpu.VMEM((4, 24, 16, 128), F32)],
        flops=1024 * 1024,
    )(active)
    taken, activation = lax.optimization_barrier((taken, activation))
    terms = spread((kept + taken).astype(BF16), ("x", "y"))
    sums = call(chip_sum_kernel, shape((N_DP, 1, WIDTH), F32))(terms)
    copies = call(scene_sum_kernel, shape((N_BRICK, 1, WIDTH), F32))(spread(sums, "dp"))
    grad = call(unpack_kernel, shape((C_OUT, SHARD), F32), [pltpu.VMEM((ROWS, 128), F32)])(
        spread(copies, BRICK)
    )
    return activation.reshape(cotangent.shape), grad.T


def solution(mesh):
    fine = jax.sharding.Mesh(mesh.devices.reshape(N_DP, 4, 8, 2), ("dp", "x", "y", "core"))
    placed = (
        P(("dp",) + BRICK, None, None, None),
        P(("dp",) + BRICK, None, None),
        P("dp", None),
        P("dp", BRICK, None, None),
    )
    return jax.shard_map(
        body,
        mesh=fine,
        in_specs=placed,
        out_specs=(P("dp", BRICK, None, None), P("dp", None)),
        check_vma=False,
    )
```
